128 devices in a mesh: grp: 2 (over core), dp: 32 (over x_hi, z, y), mp: 2 (over x_lo).
Axes of the slice: x: 4 (x_hi: 2, x_lo: 2; x = x_hi * 2 + x_lo), y: 4, z: 4, core: 2. Of those that a mesh axis runs over, the one named last changes fastest.
Arguments:
- hidden_in: bfloat16 [2, 8192, 2048], P('grp', 'dp'), may hold values from -6 to 6
- norm_gain: bfloat16 [2, 2048], P('grp'), may hold values from 0.099609375 to 1.8984375
- router: bfloat16 [2, 2048, 32], P('grp'), may hold values from -0.125 to 0.125
- routes: int32 [2, 8192, 2], P('grp', 'dp'), may hold values from 0 to 31, all different within a row; in each aligned block of 256 rows (0 to 255, 256 to 511, ..., all dimensions but the last counted through in order) at most 32 rows name the same one
- expert_in: bfloat16 [2, 32, 2048, 4096], P('grp', 'dp', None, 'mp'), may hold values from -0.125 to 0.125
- expert_out: bfloat16 [2, 32, 4096, 2048], P('grp', 'dp', 'mp'), may hold values from -0.09375 to 0.09375
- attn_weight: bfloat16 [2, 2, 2048, 1024], P('grp', None, None, 'mp'), may hold values from -0.125 to 0.125
- src_segments: int32 [32, 256], P('dp'), may hold values from 0 to 7, never falling along the last dimension, each value on 1 to 128 neighbouring positions
- tgt_segments: int32 [32, 256], P('dp'), may hold values from 0 to 7, never falling along the last dimension, each value on 1 to 128 neighbouring positions
- cotangent: bfloat16 [8192, 2048], P('dp'), may hold values from -6 to 6
Outputs:
- layer_out: bfloat16 [2, 8192, 2048], P('grp', 'dp', 'mp')
- input_grad: bfloat16 [2, 8192, 2048], P('grp', 'dp', 'mp')
The draws below stay inside these ranges and needn't reach their ends.
Inputs may be any that keep to these rules, and one draw needn't show every extreme that they name: `routes`: each row names two different experts. Within the 256 rows of one batch row of one group no expert is named by more than 32 rows, and in every draw some expert is named by exactly 32 rows of some batch row. `src_segments`: in each row the numbers never fall, and each of the 8 sentences holds 1 to 128 positions, one exactly 128. `tgt_segments`: in each row the numbers never fall, and each of the 8 sentences holds 1 to 128 positions, one exactly 128.
All inputs are finite; a program needn't handle non-finite values.
Results may differ from the reference program's by a relative error of at most 0.019.
Values may be sent and summed in bfloat16 or wider, within the bound.
A program may use at most 128 MiB of HBM per device.

```python
import math
import jax
import jax.numpy as jnp
import numpy as np
from jax import lax

D = 2048
FF = 4096
HEADS = 8
HEAD_DIM = 128
SENTS = 8
TOK_DEV = 256
TOKENS = 8192
EXPERTS = 32
CAP = 32
MOST_LEN = 128
N_GRP = 2
N_DP = 32


def level_of(stream_key, shape, cuts, least, high):
    def one(position, blocks):
        draws = jax.random.uniform(jax.random.fold_in(jax.random.fold_in(stream_key, 6), position), (blocks,), jnp.float32, least / len(cuts), high / len(cuts))
        return jnp.repeat(jnp.exp(draws), shape[position] // blocks).reshape((-1,) + (1,) * (len(shape) - position - 1))

    loudness = one(*cuts[0])
    for cut in cuts[1:]:
        loudness = loudness * one(*cut)
    return loudness


def length_profile(number_of, total, reach, slope):
    loads = [(1 << 20) // math.isqrt(rank ** slope) + 1 for rank in range(2, number_of + 1)]
    rest, holding = total - reach - (number_of - 1), [1] * (number_of - 1)
    while rest > 0:
        candidates = [i for i in range(number_of - 1) if holding[i] < reach]
        whole, budget = sum([loads[i] for i in candidates]), rest
        for i in candidates:
            addition = min(reach - holding[i], max(1, budget * loads[i] // whole), rest)
            holding[i] = holding[i] + addition
            rest = rest - addition
    return np.array([reach] + holding)


def ragged_sizes(rng, amount, total, limit, lean):
    if amount == 2:
        one = jax.random.randint(rng, (), max(1, total - limit), min(limit, total - 1) + 1)
        return jnp.stack([one, total - one])
    lengths = jnp.asarray(length_profile(amount, total, limit, lean), jnp.int32)
    couples = (amount - 1) // 2
    donor, taker = lengths[1:1 + 2 * couples:2], lengths[2:2 + 2 * couples:2]
    room = jnp.minimum(donor - 1, limit - taker)
    passed = jax.random.randint(jax.random.fold_in(rng, 1), (couples,), 0, 1 << 20) % (room + 1)
    lengths = lengths.at[1:1 + 2 * couples:2].set(donor - passed).at[2:2 + 2 * couples:2].set(taker + passed)
    return lengths[jax.random.permutation(jax.random.fold_in(rng, 2), amount)]


def assign_block(own_key, own, number, rows, number_of, top, reach, slope):
    order = jax.random.permutation(own_key, number_of)
    packed, ordinary = shares(number_of, rows * top, reach, slope, True), shares(number_of, rows * top, reach, slope, False)
    places = jnp.arange(number_of)

    def named(lengths, rotation):
        used = int((lengths > 0).sum())
        fixed = max(1, used // 4)
        moved = fixed + (places - fixed + rotation * (used - fixed)) % max(1, number_of - fixed)
        return jnp.zeros((number_of,), jnp.int32).at[order[jnp.where(places < fixed, places, moved)]].set(jnp.asarray(lengths, jnp.int32))

    lengths = jnp.where(number % 4 == 0, named(packed, number // 4), named(ordinary, number - number // 4 - 1))
    mixed = jax.random.permutation(jax.random.fold_in(own, 3), number_of)
    donor, taker = mixed[0:number_of // 2 * 2:2], mixed[1:number_of // 2 * 2:2]
    slack = jnp.minimum(lengths[donor] - 1, reach - lengths[taker]) // 2
    slack = jnp.where((donor == order[0]) | (taker == order[0]) | (lengths[taker] == 0), 0, jnp.maximum(slack, 0))
    moved = jax.random.randint(jax.random.fold_in(own, 4), (number_of // 2,), 0, 1 << 20) % (slack + 1)
    lengths = lengths.at[donor].add(-moved).at[taker].add(moved)
    members = jnp.searchsorted(jnp.cumsum(lengths), jnp.arange(rows * top), side="right").astype(jnp.int32)
    listing = members.reshape(top, rows).T
    listing = listing[jax.random.permutation(jax.random.fold_in(own, 1), rows)]
    rotation = jax.random.randint(jax.random.fold_in(own, 2), (rows, 1), 0, top)
    return jnp.take_along_axis(listing, (jnp.arange(top)[None, :] + rotation) % top, axis=1)


def shares(count, total, bound, slope, full):
    weights = [(1 << 20) // math.isqrt(rank ** slope) + 1 for rank in range(1, count + 1)]
    largest = bound if full else min(bound, max(-(-total // count), total * weights[0] // sum(weights)))
    least = 1 if total - largest >= count - 1 else 0
    holding, surplus = [largest] + [least] * (count - 1), total - largest - least * (count - 1)
    while surplus > 0:
        movable = [i for i in range(1, count) if holding[i] < largest] or [i for i in range(1, count) if holding[i] < bound]
        mass, budget = sum([weights[i] for i in movable]), surplus
        for i in movable:
            more = min(bound - holding[i], max(1, budget * weights[i] // mass), surplus)
            holding[i] = holding[i] + more
            surplus = surplus - more
    return np.array(holding)


def scatter_about(key, shape, scale, limit, shards=(), kind=jnp.bfloat16):
    loudness = level_of(key, shape, shards, -0.22, 0.18) if shards else 1.0
    drawn = jax.random.normal(key, shape, jnp.float32) * scale * loudness
    return jnp.minimum(jnp.maximum(drawn, -limit), limit).astype(kind)


def setup_inputs(seed: int = 0) -> dict:
    splits = jax.random.split(jax.random.key(seed), 11)
    hidden_in = scatter_about(splits[0], (N_GRP, TOKENS, D), 1.0, 6.0, ((0, 2), (1, 32)))
    norm_gain = jnp.clip(1.0 + 0.18 * jax.random.normal(splits[1], (N_GRP, D), jnp.float32), 0.099609375, 1.8984375).astype(jnp.bfloat16)
    router = scatter_about(splits[2], (N_GRP, D, EXPERTS), D ** -0.5, 0.125, ((0, 2),))
    routes_keys = jax.random.split(jax.random.fold_in(splits[3], 1), N_GRP * TOKENS // TOK_DEV)
    routes_turns = jax.random.permutation(jax.random.fold_in(splits[3], 3), N_GRP * TOKENS // TOK_DEV)
    routes = jax.vmap(lambda own, number: assign_block(jax.random.fold_in(splits[3], 2), own, number, TOK_DEV, EXPERTS, 2, CAP, 2))(routes_keys, routes_turns).reshape((N_GRP, TOKENS, 2))
    expert_in = scatter_about(splits[4], (N_GRP, EXPERTS, D, FF), D ** -0.5, 0.125, ((0, 2), (1, 32), (3, 2)))
    expert_out = scatter_about(splits[5], (N_GRP, EXPERTS, FF, D), FF ** -0.5, 0.09375, ((0, 2), (1, 32), (2, 2)))
    attn_weight = scatter_about(splits[6], (N_GRP, 2, D, HEADS * HEAD_DIM), D ** -0.5, 0.125, ((0, 2), (3, 2)))
    src_segments = jax.vmap(lambda own: jnp.searchsorted(jnp.cumsum(ragged_sizes(own, SENTS, TOK_DEV, MOST_LEN, 2)), jnp.arange(TOK_DEV), side="right"))(jax.random.split(splits[7], N_DP)).reshape((N_DP, TOK_DEV)).astype(jnp.int32)
    tgt_segments = jax.vmap(lambda own: jnp.searchsorted(jnp.cumsum(ragged_sizes(own, SENTS, TOK_DEV, MOST_LEN, 2)), jnp.arange(TOK_DEV), side="right"))(jax.random.split(splits[8], N_DP)).reshape((N_DP, TOK_DEV)).astype(jnp.int32)
    cotangent = scatter_about(splits[9], (TOKENS, D), 1.0, 6.0, ((0, 32),))
    return {"hidden_in": hidden_in, "norm_gain": norm_gain, "router": router, "routes": routes, "expert_in": expert_in, "expert_out": expert_out, "attn_weight": attn_weight, "src_segments": src_segments, "tgt_segments": tgt_segments, "cotangent": cotangent}


def layer_norm(token_rows, gain_row):
    values = token_rows.astype(jnp.float32)
    centred = values - lax.optimization_barrier(jnp.mean(values, -1, keepdims=True))
    variance = lax.optimization_barrier(jnp.mean(centred * centred, -1, keepdims=True))
    return (centred * lax.rsqrt(variance + 1e-05) * gain_row.astype(jnp.float32)).astype(jnp.bfloat16)

def gate_pairs(normed, router_matrix, route_rows):
    logits = jnp.dot(normed, router_matrix, preferred_element_type=jnp.float32)
    expert_ids = jnp.arange(logits.shape[1], dtype=jnp.int32)
    chosen = lax.optimization_barrier(jnp.sum(jnp.where(route_rows[:, :, None] == expert_ids[None, None, :], logits[:, None, :], jnp.zeros((), logits.dtype)), -1))
    leading = jax.nn.sigmoid(chosen[:, 0] - chosen[:, 1])
    return jnp.stack([leading, 1.0 - leading], 1)

def slot_layout(route_rows, expert_count, capacity):
    token_count = route_rows.shape[0]
    flat_ids = route_rows.reshape(-1).astype(jnp.int32)
    onehot = (flat_ids[:, None] == jnp.arange(expert_count, dtype=jnp.int32)[None, :]).astype(jnp.int32)
    earlier = jnp.cumsum(onehot, 0) - onehot
    slot_rank = lax.optimization_barrier(jnp.sum(earlier * onehot, 1))
    slot_index = (flat_ids * capacity + slot_rank).astype(jnp.int32)
    pair_token = jnp.arange(2 * token_count, dtype=jnp.int32) // 2
    slot_owner = jnp.full((expert_count * capacity,), token_count, jnp.int32).at[slot_index].set(pair_token)
    return (slot_index, slot_owner)

def expert_layer(hidden, gain_row, router_matrix, route_all, weight_in, weight_out):
    normed = layer_norm(hidden, gain_row)
    blocks = normed.reshape(N_DP, TOK_DEV, D)
    route_blocks = route_all.reshape(N_DP, TOK_DEV, 2)
    slot_index, slot_owner = jax.vmap(lambda rows: slot_layout(rows, EXPERTS, CAP))(route_blocks)
    padded = jnp.concatenate([blocks, jnp.zeros((N_DP, 1, D), blocks.dtype)], 1)
    outgoing = jax.vmap(lambda table, owner: table[owner])(padded, slot_owner).reshape(N_DP, EXPERTS, CAP, D)

    def one_expert(expert_index):
        rows = outgoing[:, expert_index].reshape(N_DP * CAP, D)
        inner = jax.nn.relu(jnp.dot(rows.astype(jnp.float32), weight_in[expert_index].astype(jnp.float32), precision=lax.Precision.HIGHEST)).astype(jnp.bfloat16)
        outer = jnp.dot(inner.astype(jnp.float32), weight_out[expert_index].astype(jnp.float32), precision=lax.Precision.HIGHEST).astype(jnp.bfloat16)
        return outer.reshape(N_DP, CAP, D)
    results = lax.map(one_expert, jnp.arange(EXPERTS, dtype=jnp.int32))
    returned = jnp.transpose(results, (1, 0, 2, 3)).reshape(N_DP, EXPERTS * CAP, D)
    gates = jax.vmap(gate_pairs, in_axes=(0, None, 0))(blocks, router_matrix, route_blocks)
    picked = jax.vmap(lambda table, index: table[index])(returned, slot_index)
    picked = picked.reshape(N_DP, TOK_DEV, 2, D).astype(jnp.float32)
    mixed = lax.optimization_barrier(jnp.sum(gates[..., None] * picked, 2))
    state = hidden.reshape(N_DP, TOK_DEV, D).astype(jnp.float32) + mixed
    return state.astype(jnp.bfloat16).reshape(TOKENS, D)

def attend_block(query_heads, key_heads, value_heads, grad_heads, seg_mask):
    softmax_scale = HEAD_DIM ** (-0.5)
    query_f = query_heads.astype(jnp.float32)
    key_f = key_heads.astype(jnp.float32)
    value_f = value_heads.astype(jnp.float32)
    grad_f = grad_heads.astype(jnp.float32)
    scores = jnp.einsum('qhd,khd->hqk', query_f, key_f) * softmax_scale
    exp_scores = jnp.exp(scores) * seg_mask[None]
    weights = exp_scores / lax.optimization_barrier(jnp.sum(exp_scores, -1, keepdims=True))
    weights_b = weights.astype(jnp.bfloat16)
    weights_bf = weights_b.astype(jnp.float32)
    context = jnp.einsum('hqk,khd->qhd', weights_bf, value_f).astype(jnp.bfloat16)
    prob_grad = jnp.einsum('qhd,khd->hqk', grad_f, value_f)
    row_delta = lax.optimization_barrier(jnp.sum(weights * prob_grad, -1, keepdims=True))
    score_grad = (weights * (prob_grad - row_delta)).astype(jnp.bfloat16).astype(jnp.float32)
    query_grad = (jnp.einsum('hqk,khd->qhd', score_grad, key_f) * softmax_scale).astype(jnp.bfloat16)
    key_grad = (jnp.einsum('hqk,qhd->khd', score_grad, query_f) * softmax_scale).astype(jnp.bfloat16)
    value_grad = jnp.einsum('hqk,qhd->khd', weights_bf, grad_f).astype(jnp.bfloat16)
    token_count = query_heads.shape[0]
    return (context.reshape(token_count, -1), query_grad.reshape(token_count, -1), key_grad.reshape(token_count, -1), value_grad.reshape(token_count, -1))

def heads_of(flat_rows):
    return flat_rows.reshape(N_DP, TOK_DEV, HEADS, HEAD_DIM)

def rows_of(block_rows):
    return block_rows.reshape(TOKENS, HEADS * HEAD_DIM)

def reference(hidden_in, norm_gain, router, routes, expert_in, expert_out, attn_weight, src_segments, tgt_segments, cotangent):
    encoded = expert_layer(hidden_in[0], norm_gain[0], router[0], routes[0], expert_in[0], expert_out[0])
    decoded = expert_layer(hidden_in[1], norm_gain[1], router[1], routes[1], expert_in[1], expert_out[1])
    key_weight = attn_weight[0, 0]
    value_weight = attn_weight[0, 1]
    query_weight = attn_weight[1, 0]
    out_weight = attn_weight[1, 1]
    keys = jnp.dot(encoded, key_weight, preferred_element_type=jnp.float32).astype(jnp.bfloat16)
    values = jnp.dot(encoded, value_weight, preferred_element_type=jnp.float32).astype(jnp.bfloat16)
    queries = jnp.dot(decoded, query_weight, preferred_element_type=jnp.float32).astype(jnp.bfloat16)
    context_grad = jnp.dot(cotangent, out_weight, preferred_element_type=jnp.float32).astype(jnp.bfloat16)
    seg_mask = (tgt_segments[:, :, None] == src_segments[:, None, :]).astype(jnp.float32)
    context, query_grad, key_grad, value_grad = jax.vmap(attend_block)(heads_of(queries), heads_of(keys), heads_of(values), heads_of(context_grad), seg_mask)
    context = rows_of(context)
    query_grad = rows_of(query_grad)
    key_grad = rows_of(key_grad)
    value_grad = rows_of(value_grad)
    layer_dec = (decoded.astype(jnp.float32) + jnp.dot(context, out_weight.T, preferred_element_type=jnp.float32)).astype(jnp.bfloat16)
    grad_enc = (jnp.dot(key_grad, key_weight.T, preferred_element_type=jnp.float32) + jnp.dot(value_grad, value_weight.T, preferred_element_type=jnp.float32)).astype(jnp.bfloat16)
    grad_dec = (cotangent.astype(jnp.float32) + jnp.dot(query_grad, query_weight.T, preferred_element_type=jnp.float32)).astype(jnp.bfloat16)
    return (jnp.stack([encoded, layer_dec]), jnp.stack([grad_enc, grad_dec]))
```

```python
import jax
import jax.numpy as jnp
from jax import lax
from jax.sharding import PartitionSpec as P

HEAD_DIM = 128


def passed_along(value, axis, by):
    peers = lax.axis_size(axis)
    pairs = [(i, i + by) for i in range(peers) if 0 <= i + by < peers]
    return lax.ppermute(value, axis, pairs)


def layer_norm(token_rows, gain_row):
    values = token_rows.astype(jnp.float32)
    centred = values - jnp.mean(values, -1, keepdims=True)
    variance = jnp.mean(centred * centred, -1, keepdims=True)
    return (centred * lax.rsqrt(variance + 1e-05) * gain_row.astype(jnp.float32)).astype(
        jnp.bfloat16
    )


def gate_pairs(normed, router_matrix, route_rows):
    logits = jnp.dot(normed, router_matrix, preferred_element_type=jnp.float32)
    expert_ids = jnp.arange(logits.shape[1], dtype=jnp.int32)
    chosen = jnp.sum(
        jnp.where(
            route_rows[:, :, None] == expert_ids[None, None, :],
            logits[:, None, :],
            jnp.zeros((), logits.dtype),
        ),
        -1,
    )
    leading = jax.nn.sigmoid(chosen[:, 0] - chosen[:, 1])
    return jnp.stack([leading, 1.0 - leading], 1)


def slot_tables(route_rows, expert_count, capacity):
    token_count = route_rows.shape[0]
    expert_ids = jnp.arange(expert_count, dtype=jnp.int32)
    hits = (route_rows[:, :, None] == expert_ids[None, None, :]).astype(jnp.bfloat16)
    token_ids = jnp.arange(token_count)
    below = (token_ids[:, None] > token_ids[None, :]).astype(jnp.bfloat16)
    earlier = jnp.dot(below, hits.sum(1), preferred_element_type=jnp.float32)
    rank = jnp.sum(earlier[:, None, :] * hits.astype(jnp.float32), -1).astype(jnp.int32)
    slots = route_rows * capacity + rank
    slot_ids = jnp.arange(expert_count * capacity, dtype=jnp.int32)
    return slots[:, :, None] == slot_ids[None, None, :]


def swapped(value):
    return lax.ppermute(value, "mp", [(0, 1), (1, 0)])


def contract_rows(left_rows, weight):
    return lax.dot_general(
        left_rows, weight, (((1,), (1,)), ((), ())), preferred_element_type=jnp.float32
    )


def cross_attend(query_rows, key_rows, value_rows, seg_mask, cot_rows, query_weight, out_weight):
    token_count = query_rows.shape[0]
    source_count = key_rows.shape[0]
    head_count = query_rows.shape[1] // HEAD_DIM
    softmax_scale = HEAD_DIM ** (-0.5)
    query_heads = query_rows.reshape(token_count, head_count, HEAD_DIM)
    key_heads = key_rows.reshape(source_count, head_count, HEAD_DIM)
    value_heads = value_rows.reshape(source_count, head_count, HEAD_DIM)
    scores = (
        jnp.einsum("qhd,khd->hqk", query_heads, key_heads, preferred_element_type=jnp.float32)
        * softmax_scale
    )
    exp_scores = jnp.exp(scores) * seg_mask[None]
    weights = exp_scores / jnp.sum(exp_scores, -1, keepdims=True)
    weights_b = weights.astype(jnp.bfloat16)
    context = jnp.einsum(
        "hqk,khd->qhd", weights_b, value_heads, preferred_element_type=jnp.float32
    ).astype(jnp.bfloat16)
    out_term = contract_rows(context.reshape(token_count, -1), out_weight)
    context_grad = jnp.dot(cot_rows, out_weight, preferred_element_type=jnp.float32).astype(
        jnp.bfloat16
    )
    grad_heads = context_grad.reshape(token_count, head_count, HEAD_DIM)
    prob_grad = jnp.einsum(
        "qhd,khd->hqk", grad_heads, value_heads, preferred_element_type=jnp.float32
    )
    row_delta = jnp.sum(weights * prob_grad, -1, keepdims=True)
    score_grad = (weights * (prob_grad - row_delta)).astype(jnp.bfloat16)
    query_grad = (
        jnp.einsum("hqk,khd->qhd", score_grad, key_heads, preferred_element_type=jnp.float32)
        * softmax_scale
    ).astype(jnp.bfloat16)
    key_grad = (
        jnp.einsum("hqk,qhd->khd", score_grad, query_heads, preferred_element_type=jnp.float32)
        * softmax_scale
    ).astype(jnp.bfloat16)
    value_grad = jnp.einsum(
        "hqk,qhd->khd", weights_b, grad_heads, preferred_element_type=jnp.float32
    ).astype(jnp.bfloat16)
    query_term = contract_rows(query_grad.reshape(token_count, -1), query_weight)
    key_value_grads = jnp.stack(
        [key_grad.reshape(source_count, -1), value_grad.reshape(source_count, -1)]
    )
    return (out_term, query_term, key_value_grads)


def per_device(
    hidden_in,
    norm_gain,
    router,
    routes,
    expert_in,
    expert_out,
    attn_weight,
    src_segments,
    tgt_segments,
    cotangent,
):
    group_index = lax.axis_index("grp")
    mp_index = lax.axis_index("mp")
    expert_count = lax.axis_size("dp")
    token_rows = hidden_in[0]
    token_count, model_width = token_rows.shape
    capacity = 4 * token_count // expert_count
    half_width = model_width // lax.axis_size("mp")
    normed = layer_norm(token_rows, norm_gain[0])
    route_rows = routes[0]
    gate_rows = gate_pairs(normed, router[0], route_rows)
    places = slot_tables(route_rows, expert_count, capacity)
    weight_in = expert_in[0, 0]
    weight_out = expert_out[0, 0]
    outgoing = lax.dot_general(
        places.any(1).astype(jnp.bfloat16),
        normed,
        (((0,), (0,)), ((), ())),
        preferred_element_type=jnp.float32,
    ).astype(jnp.bfloat16)
    outgoing = outgoing.reshape(expert_count, capacity, model_width)
    arrived = lax.all_to_all(outgoing, "dp", split_axis=0, concat_axis=0, tiled=True)
    slot_count = arrived.shape[1]
    expert_inner = jax.nn.relu(
        jnp.dot(arrived.reshape(-1, model_width), weight_in, preferred_element_type=jnp.float32)
    ).astype(jnp.bfloat16)
    expert_term = jnp.dot(expert_inner, weight_out, preferred_element_type=jnp.float32)
    result_rows = expert_term.astype(jnp.bfloat16).reshape(arrived.shape)
    returned_rows = lax.all_to_all(result_rows, "dp", split_axis=0, concat_axis=0, tiled=True)
    returned_rows = returned_rows.reshape(expert_count * capacity, model_width)
    mixing = jnp.sum(jnp.where(places, gate_rows[:, :, None], 0.0), 1)
    coarse = mixing.astype(jnp.bfloat16)
    fine = (mixing - coarse.astype(jnp.float32)).astype(jnp.bfloat16)
    mixed_rows = jnp.dot(coarse, returned_rows, preferred_element_type=jnp.float32) + jnp.dot(
        fine, returned_rows, preferred_element_type=jnp.float32
    )

    def own_half(value):
        return lax.dynamic_slice_in_dim(value, mp_index * half_width, half_width, 1)

    def other_half(value):
        return lax.dynamic_slice_in_dim(value, (1 - mp_index) * half_width, half_width, 1)

    mixed_half = own_half(mixed_rows) + swapped(other_half(mixed_rows).astype(jnp.bfloat16)).astype(jnp.float32)
    state_half = (own_half(token_rows).astype(jnp.float32) + mixed_half).astype(jnp.bfloat16)
    state_other = swapped(state_half)
    layer_state = jnp.where(
        mp_index == 0,
        jnp.concatenate([state_half, state_other], 1),
        jnp.concatenate([state_other, state_half], 1),
    )
    proj_first = attn_weight[0, 0]
    proj_second = attn_weight[0, 1]
    projected = jnp.dot(layer_state, proj_first, preferred_element_type=jnp.float32).astype(
        jnp.bfloat16
    )

    def encoder_values():
        return jnp.dot(layer_state, proj_second, preferred_element_type=jnp.float32).astype(
            jnp.bfloat16
        )

    def absent_values():
        return jnp.zeros_like(projected)

    value_rows = lax.cond(group_index == 0, encoder_values, absent_values)
    handed = passed_along(jnp.stack([projected, value_rows]), "grp", 1)
    seg_mask = (tgt_segments[0][:, None] == src_segments[0][None, :]).astype(jnp.float32)

    def decoder_side():
        return cross_attend(
            projected, handed[0], handed[1], seg_mask, cotangent, proj_first, proj_second
        )

    def encoder_side():
        zero_rows = jnp.zeros((token_count, model_width), jnp.float32)
        return (zero_rows, zero_rows, jnp.zeros_like(handed))

    out_term, query_term, key_value_grads = lax.cond(group_index == 1, decoder_side, encoder_side)
    grads_in = passed_along(key_value_grads, "grp", -1)

    def encoder_grad():
        return contract_rows(grads_in[0], proj_first) + contract_rows(grads_in[1], proj_second)

    def decoder_grad():
        return query_term

    grad_term = lax.cond(group_index == 0, encoder_grad, decoder_grad)
    out_share = own_half(out_term) + swapped(other_half(out_term).astype(jnp.bfloat16)).astype(jnp.float32)
    grad_share = own_half(grad_term) + swapped(other_half(grad_term).astype(jnp.bfloat16)).astype(jnp.float32)
    cot_half = lax.dynamic_slice_in_dim(cotangent, mp_index * half_width, half_width, 1)
    forward = jnp.where(
        group_index == 0,
        state_half,
        (state_half.astype(jnp.float32) + out_share).astype(jnp.bfloat16),
    )
    backward = jnp.where(
        group_index == 0,
        grad_share.astype(jnp.bfloat16),
        (cot_half.astype(jnp.float32) + grad_share).astype(jnp.bfloat16),
    )
    return (forward[None], backward[None])


def solution(mesh):
    return jax.shard_map(
        per_device,
        mesh=mesh,
        in_specs=(
            P("grp", "dp", None),
            P("grp", None),
            P("grp", None, None),
            P("grp", "dp", None),
            P("grp", "dp", None, "mp"),
            P("grp", "dp", "mp", None),
            P("grp", None, None, "mp"),
            P("dp", None),
            P("dp", None),
            P("dp", None),
        ),
        out_specs=(P("grp", "dp", "mp"), P("grp", "dp", "mp")),
        check_vma=False,
    )
```

```python
import jax
import jax.numpy as jnp
from jax import lax
from jax.experimental import pallas as pl
from jax.experimental.pallas import tpu as pltpu
from jax.sharding import PartitionSpec as P

HEAD_DIM = 128


def passed_along(value, axis, by):
    peers = lax.axis_size(axis)
    pairs = [(i, i + by) for i in range(peers) if 0 <= i + by < peers]
    return lax.ppermute(value, axis, pairs)


def layer_norm(token_rows, gain_row):
    values = token_rows.astype(jnp.float32)
    centred = values - jnp.mean(values, -1, keepdims=True)
    variance = jnp.mean(centred * centred, -1, keepdims=True)
    return (centred * lax.rsqrt(variance + 1e-05) * gain_row.astype(jnp.float32)).astype(
        jnp.bfloat16
    )


def gate_pairs(normed, router_matrix, route_rows):
    logits = jnp.dot(normed, router_matrix, preferred_element_type=jnp.float32)
    expert_ids = jnp.arange(logits.shape[1], dtype=jnp.int32)
    chosen = jnp.sum(
        jnp.where(
            route_rows[:, :, None] == expert_ids[None, None, :],
            logits[:, None, :],
            jnp.zeros((), logits.dtype),
        ),
        -1,
    )
    leading = jax.nn.sigmoid(chosen[:, 0] - chosen[:, 1])
    return jnp.stack([leading, 1.0 - leading], 1)


def slot_tables(route_rows, expert_count, capacity):
    token_count = route_rows.shape[0]
    expert_ids = jnp.arange(expert_count, dtype=jnp.int32)
    hits = (route_rows[:, :, None] == expert_ids[None, None, :]).astype(jnp.bfloat16)
    token_ids = jnp.arange(token_count)
    below = (token_ids[:, None] > token_ids[None, :]).astype(jnp.bfloat16)
    earlier = jnp.dot(below, hits.sum(1), preferred_element_type=jnp.float32)
    rank = jnp.sum(earlier[:, None, :] * hits.astype(jnp.float32), -1).astype(jnp.int32)
    slots = route_rows * capacity + rank
    slot_ids = jnp.arange(expert_count * capacity, dtype=jnp.int32)
    return slots[:, :, None] == slot_ids[None, None, :]


def swapped(value):
    return lax.ppermute(value, "mp", [(0, 1), (1, 0)])


RINGS = (2, 4, 4)
SHARE = 512
BOTH = 1024
GROUP = 128
BLOCK = 256
TILE = 256


def shortest(offset):
    return sum(min(step, ring - step) for step, ring in zip(offset, RINGS))


OFFSETS = sorted(
    [(h, z, y) for h in range(RINGS[0]) for z in range(RINGS[1]) for y in range(RINGS[2])],
    key=shortest,
)


def expert_kernel(
    outgoing,
    first_hbm,
    second_hbm,
    returned,
    arrived,
    inner,
    first,
    second,
    for_partner,
    from_partner,
    both,
    share,
    load_sem,
    own_sem,
    send_sem,
    recv_sem,
    pass_sem,
    passed_sem,
    half_sem,
    halved_sem,
    back_sem,
    came_sem,
):
    row, mp = lax.axis_index("dp"), lax.axis_index("mp")
    cap = outgoing.shape[0] // len(OFFSETS)
    width = outgoing.shape[1]
    row_h, row_z, row_y = row // 16, row // 4 % 4, row % 4

    def place(offset, sign):
        dh, dz, dy = offset
        index = (
            (row_h + dh) % 2 * 16 + (row_z + sign * dz + 4) % 4 * 4 + (row_y + sign * dy + 4) % 4
        )
        return index, (mp + dh) % 2

    def device(index, side):
        return {"dp": index, "mp": side}

    partner = device(row, 1 - mp)
    barrier = pltpu.get_barrier_semaphore()
    for offset in OFFSETS[1:]:
        pl.semaphore_signal(barrier, inc=1, device_id=device(*place(offset, -1)), device_id_type=pl.DeviceIdType.MESH)
    pl.semaphore_signal(barrier, inc=1, device_id=partner, device_id_type=pl.DeviceIdType.MESH)

    loads = [
        pltpu.make_async_copy(first_hbm, first, load_sem.at[0]),
        pltpu.make_async_copy(second_hbm, second, load_sem.at[1]),
    ]
    for load in loads:
        load.start()
    pl.semaphore_wait(barrier, len(OFFSETS))

    def remote(source, target, sent, landed, where):
        return pltpu.make_async_remote_copy(
            source, target, sent, landed, device_id=where, device_id_type=pl.DeviceIdType.MESH
        )

    def dispatch(slot, side, index, where):
        columns = pl.ds(pl.multiple_of(side * SHARE, SHARE), SHARE + BOTH)
        source = outgoing.at[pl.ds(pl.multiple_of(index * cap, cap), cap), columns]
        target = arrived.at[pl.ds(slot * cap, cap), columns]
        if slot == 0:
            return pltpu.make_async_copy(source, target, own_sem.at[0])
        return remote(source, target, send_sem.at[slot], recv_sem.at[slot], where)

    sends = []
    for slot, offset in enumerate(OFFSETS):
        index, side = place(offset, 1)
        sends.append(dispatch(slot, side, index, device(index, side)))
        sends[slot].start()

    def wait_arrival(slot):
        if slot == 0:
            sends[0].wait()
        else:
            dispatch(slot, mp, row, partner).wait_recv()

    own_start = pl.multiple_of(mp * (SHARE + BOTH), SHARE)
    their_start = pl.multiple_of((1 - mp) * (SHARE + BOTH), SHARE)

    def forward(group, start):
        region = arrived.at[pl.ds(group * GROUP, GROUP), pl.ds(start, SHARE)]
        return remote(region, region, pass_sem.at[group], passed_sem.at[group], partner)

    def up_project(block):
        rows = pl.ds(block * BLOCK, BLOCK)

        def step(tile, carry):
            columns = pl.ds(pl.multiple_of(tile * TILE, TILE), TILE)
            product = jnp.dot(arrived[rows, :], first[:, columns], preferred_element_type=jnp.float32)
            inner[rows, columns] = jnp.maximum(product, 0.0).astype(jnp.bfloat16)
            return carry

        lax.fori_loop(0, inner.shape[1] // TILE, step, 0)

    groups = arrived.shape[0] // GROUP
    blocks = arrived.shape[0] // BLOCK
    per_group = GROUP // cap
    per_block = BLOCK // cap
    forwards = [forward(group, own_start) for group in range(groups)]
    for block in range(blocks + 1):
        if block < blocks:
            for group in range(block * BLOCK // GROUP, (block + 1) * BLOCK // GROUP):
                for slot in range(group * per_group, (group + 1) * per_group):
                    wait_arrival(slot)
                forwards[group].start()
        if block == 1:
            loads[0].wait()
        if block > 0:
            for group in range((block - 1) * BLOCK // GROUP, block * BLOCK // GROUP):
                forward(group, their_start).wait_recv()
            up_project(block - 1)

    def down_project(block, start, count, finish):
        rows = pl.ds(block * BLOCK, BLOCK)

        def step(tile, carry):
            columns = pl.ds(pl.multiple_of(start + tile * TILE, TILE), TILE)
            product = jnp.dot(inner[rows, :], second[:, columns], preferred_element_type=jnp.float32)
            finish(rows, pl.ds(pl.multiple_of(tile * TILE, TILE), TILE), product)
            return carry

        lax.fori_loop(0, count // TILE, step, 0)

    def keep_in(buffer):
        def finish(rows, columns, product):
            buffer[rows, columns] = product.astype(jnp.bfloat16)

        return finish

    def add_share(rows, columns, product):
        total = product + from_partner[rows, columns].astype(jnp.float32)
        share[rows, columns] = total.astype(jnp.bfloat16)

    def halve(block):
        rows = pl.ds(block * BLOCK, BLOCK)
        return remote(for_partner.at[rows], from_partner.at[rows], half_sem.at[block], halved_sem.at[block], partner)

    def give_back(slot, part, expert, where):
        buffer, start, count = ((both, 0, BOTH), (share, BOTH, SHARE))[part]
        source = buffer.at[pl.ds(slot * cap, cap)]
        target = returned.at[pl.ds(pl.multiple_of(expert * cap, cap), cap), pl.ds(start, count)]
        if slot == 0:
            return pltpu.make_async_copy(source, target, own_sem.at[1 + part])
        number = part * len(OFFSETS) + slot
        return remote(source, target, back_sem.at[number], came_sem.at[number], where)

    backs = []

    def give_block_back(block, part):
        for slot in range(block * per_block, (block + 1) * per_block):
            back = give_back(slot, part, row, device(*place(OFFSETS[slot], -1)))
            back.start()
            backs.append((slot, back))

    loads[1].wait()
    halves = [halve(block) for block in range(blocks)]
    for block in range(blocks):
        down_project(block, their_start, SHARE, keep_in(for_partner))
        halves[block].start()
    for block in range(blocks):
        down_project(block, SHARE, BOTH, keep_in(both))
        give_block_back(block, 0)
    for block in range(blocks):
        halves[block].wait_recv()
        down_project(block, own_start, SHARE, add_share)
        give_block_back(block, 1)

    for part in range(2):
        for slot in range(1, len(OFFSETS)):
            give_back(slot, part, place(OFFSETS[slot], 1)[0], partner).wait_recv()
    for slot, back in backs:
        if slot == 0:
            back.wait()
        else:
            back.wait_send()
    for slot in range(1, len(OFFSETS)):
        sends[slot].wait_send()
    for copy in forwards + halves:
        copy.wait_send()


def expert_exchange(outgoing, first, second):
    slots, width = outgoing.shape
    hidden = first.shape[1]
    count = len(OFFSETS)
    groups, blocks = slots // GROUP, slots // BLOCK
    dma = pltpu.SemaphoreType.DMA
    return pl.pallas_call(
        expert_kernel,
        out_shape=jax.ShapeDtypeStruct((slots, BOTH + SHARE), jnp.bfloat16),
        in_specs=[
            pl.BlockSpec(memory_space=pltpu.VMEM),
            pl.BlockSpec(memory_space=pl.ANY),
            pl.BlockSpec(memory_space=pl.ANY),
        ],
        out_specs=pl.BlockSpec(memory_space=pl.ANY),
        scratch_shapes=[
            pltpu.VMEM((slots, width), jnp.bfloat16),
            pltpu.VMEM((slots, hidden), jnp.bfloat16),
            pltpu.VMEM(first.shape, jnp.bfloat16),
            pltpu.VMEM(second.shape, jnp.bfloat16),
            pltpu.VMEM((slots, SHARE), jnp.bfloat16),
            pltpu.VMEM((slots, SHARE), jnp.bfloat16),
            pltpu.VMEM((slots, BOTH), jnp.bfloat16),
            pltpu.VMEM((slots, SHARE), jnp.bfloat16),
            dma((2,)),
            dma((3,)),
            dma((count,)),
            dma((count,)),
            dma((groups,)),
            dma((groups,)),
            dma((blocks,)),
            dma((blocks,)),
            dma((2 * count,)),
            dma((2 * count,)),
        ],
        compiler_params=pltpu.CompilerParams(
            collective_id=0, has_side_effects=True, vmem_limit_bytes=56 * 1024 * 1024
        ),
        cost_estimate=pl.CostEstimate(
            flops=4 * slots * width * hidden, bytes_accessed=24 * 1024 * 1024, transcendentals=0
        ),
        name="expert_exchange",
    )(outgoing, first, second)


def contract_rows(left_rows, weight):
    return lax.dot_general(
        left_rows, weight, (((1,), (1,)), ((), ())), preferred_element_type=jnp.float32
    )


def cross_attend(query_rows, key_rows, value_rows, seg_mask, cot_rows, query_weight, out_weight):
    token_count = query_rows.shape[0]
    source_count = key_rows.shape[0]
    head_count = query_rows.shape[1] // HEAD_DIM
    softmax_scale = HEAD_DIM ** (-0.5)
    query_heads = query_rows.reshape(token_count, head_count, HEAD_DIM)
    key_heads = key_rows.reshape(source_count, head_count, HEAD_DIM)
    value_heads = value_rows.reshape(source_count, head_count, HEAD_DIM)
    scores = (
        jnp.einsum("qhd,khd->hqk", query_heads, key_heads, preferred_element_type=jnp.float32)
        * softmax_scale
    )
    exp_scores = jnp.exp(scores) * seg_mask[None]
    weights = exp_scores / jnp.sum(exp_scores, -1, keepdims=True)
    weights_b = weights.astype(jnp.bfloat16)
    context = jnp.einsum(
        "hqk,khd->qhd", weights_b, value_heads, preferred_element_type=jnp.float32
    ).astype(jnp.bfloat16)
    out_term = contract_rows(context.reshape(token_count, -1), out_weight)
    context_grad = jnp.dot(cot_rows, out_weight, preferred_element_type=jnp.float32).astype(
        jnp.bfloat16
    )
    grad_heads = context_grad.reshape(token_count, head_count, HEAD_DIM)
    prob_grad = jnp.einsum(
        "qhd,khd->hqk", grad_heads, value_heads, preferred_element_type=jnp.float32
    )
    row_delta = jnp.sum(weights * prob_grad, -1, keepdims=True)
    score_grad = (weights * (prob_grad - row_delta)).astype(jnp.bfloat16)
    query_grad = (
        jnp.einsum("hqk,khd->qhd", score_grad, key_heads, preferred_element_type=jnp.float32)
        * softmax_scale
    ).astype(jnp.bfloat16)
    key_grad = (
        jnp.einsum("hqk,qhd->khd", score_grad, query_heads, preferred_element_type=jnp.float32)
        * softmax_scale
    ).astype(jnp.bfloat16)
    value_grad = jnp.einsum(
        "hqk,qhd->khd", weights_b, grad_heads, preferred_element_type=jnp.float32
    ).astype(jnp.bfloat16)
    query_term = contract_rows(query_grad.reshape(token_count, -1), query_weight)
    key_value_grads = jnp.stack(
        [key_grad.reshape(source_count, -1), value_grad.reshape(source_count, -1)]
    )
    return (out_term, query_term, key_value_grads)


def per_device(
    hidden_in,
    norm_gain,
    router,
    routes,
    expert_in,
    expert_out,
    attn_weight,
    src_segments,
    tgt_segments,
    cotangent,
):
    group_index = lax.axis_index("grp")
    mp_index = lax.axis_index("mp")
    expert_count = lax.axis_size("dp")
    token_rows = hidden_in[0]
    token_count, model_width = token_rows.shape
    capacity = 4 * token_count // expert_count
    half_width = model_width // lax.axis_size("mp")
    normed = layer_norm(token_rows, norm_gain[0])
    route_rows = routes[0]
    gate_rows = gate_pairs(normed, router[0], route_rows)
    places = slot_tables(route_rows, expert_count, capacity)
    weight_in = expert_in[0, 0]
    weight_out = expert_out[0, 0]
    outgoing = lax.dot_general(
        places.any(1).astype(jnp.bfloat16),
        normed,
        (((0,), (0,)), ((), ())),
        preferred_element_type=jnp.float32,
    ).astype(jnp.bfloat16)
    returned = expert_exchange(outgoing, weight_in, weight_out)
    mixing = jnp.sum(jnp.where(places, gate_rows[:, :, None], 0.0), 1)
    coarse = mixing.astype(jnp.bfloat16)
    fine = (mixing - coarse.astype(jnp.float32)).astype(jnp.bfloat16)

    def mixed(weights, rows):
        return jnp.dot(weights, rows, preferred_element_type=jnp.float32)

    half_slots = expert_count * capacity // 2
    my_side = lax.axis_index("dp") // (expert_count // 2)

    def side_of(value, side, axis):
        return lax.dynamic_slice_in_dim(value, side * half_slots, half_slots, axis)

    def mixed_share(side):
        rows = side_of(returned[:, BOTH:], side, 0)
        return mixed(side_of(coarse, side, 1), rows) + mixed(side_of(fine, side, 1), rows)

    mixed_both = mixed(coarse, returned[:, :BOTH]) + mixed(fine, returned[:, :BOTH])
    mixed_own, mixed_other = mixed_share(my_side), mixed_share(1 - my_side)
    mixed_rows = jnp.where(
        mp_index == 0,
        jnp.concatenate([mixed_own, mixed_both, mixed_other], 1),
        jnp.concatenate([mixed_other, mixed_both, mixed_own], 1),
    )

    def own_half(value):
        return lax.dynamic_slice_in_dim(value, mp_index * half_width, half_width, 1)

    def other_half(value):
        return lax.dynamic_slice_in_dim(value, (1 - mp_index) * half_width, half_width, 1)

    mixed_half = own_half(mixed_rows) + swapped(other_half(mixed_rows).astype(jnp.bfloat16)).astype(jnp.float32)
    state_half = (own_half(token_rows).astype(jnp.float32) + mixed_half).astype(jnp.bfloat16)
    state_other = swapped(state_half)
    layer_state = jnp.where(
        mp_index == 0,
        jnp.concatenate([state_half, state_other], 1),
        jnp.concatenate([state_other, state_half], 1),
    )
    proj_first = attn_weight[0, 0]
    proj_second = attn_weight[0, 1]
    projected = jnp.dot(layer_state, proj_first, preferred_element_type=jnp.float32).astype(
        jnp.bfloat16
    )

    def encoder_values():
        return jnp.dot(layer_state, proj_second, preferred_element_type=jnp.float32).astype(
            jnp.bfloat16
        )

    def absent_values():
        return jnp.zeros_like(projected)

    value_rows = lax.cond(group_index == 0, encoder_values, absent_values)
    handed = passed_along(jnp.stack([projected, value_rows]), "grp", 1)
    seg_mask = (tgt_segments[0][:, None] == src_segments[0][None, :]).astype(jnp.float32)

    def decoder_side():
        return cross_attend(
            projected, handed[0], handed[1], seg_mask, cotangent, proj_first, proj_second
        )

    def encoder_side():
        zero_rows = jnp.zeros((token_count, model_width), jnp.float32)
        return (zero_rows, zero_rows, jnp.zeros_like(handed))

    out_term, query_term, key_value_grads = lax.cond(group_index == 1, decoder_side, encoder_side)
    grads_in = passed_along(key_value_grads, "grp", -1)

    def encoder_grad():
        return contract_rows(grads_in[0], proj_first) + contract_rows(grads_in[1], proj_second)

    def decoder_grad():
        return query_term

    grad_term = lax.cond(group_index == 0, encoder_grad, decoder_grad)
    out_share = own_half(out_term) + swapped(other_half(out_term).astype(jnp.bfloat16)).astype(jnp.float32)
    grad_share = own_half(grad_term) + swapped(other_half(grad_term).astype(jnp.bfloat16)).astype(jnp.float32)
    cot_half = lax.dynamic_slice_in_dim(cotangent, mp_index * half_width, half_width, 1)
    forward = jnp.where(
        group_index == 0,
        state_half,
        (state_half.astype(jnp.float32) + out_share).astype(jnp.bfloat16),
    )
    backward = jnp.where(
        group_index == 0,
        grad_share.astype(jnp.bfloat16),
        (cot_half.astype(jnp.float32) + grad_share).astype(jnp.bfloat16),
    )
    return (forward[None], backward[None])


def solution(mesh):
    return jax.shard_map(
        per_device,
        mesh=mesh,
        in_specs=(
            P("grp", "dp", None),
            P("grp", None),
            P("grp", None, None),
            P("grp", "dp", None),
            P("grp", "dp", None, "mp"),
            P("grp", "dp", "mp", None),
            P("grp", None, None, "mp"),
            P("dp", None),
            P("dp", None),
            P("dp", None),
        ),
        out_specs=(P("grp", "dp", "mp"), P("grp", "dp", "mp")),
        check_vma=False,
    )
```

```python
import jax
import jax.numpy as jnp
from jax import lax
from jax.experimental import pallas as pl
from jax.experimental.pallas import tpu as pltpu
from jax.sharding import PartitionSpec as P

HEAD_DIM = 128


def layer_norm(token_rows, gain_row):
    values = token_rows.astype(jnp.float32)
    centred = values - jnp.mean(values, -1, keepdims=True)
    variance = jnp.mean(centred * centred, -1, keepdims=True)
    return (centred * lax.rsqrt(variance + 1e-05) * gain_row.astype(jnp.float32)).astype(
        jnp.bfloat16
    )


def gate_pairs(normed, router_matrix, route_rows):
    logits = jnp.dot(normed, router_matrix, preferred_element_type=jnp.float32)
    expert_ids = jnp.arange(logits.shape[1], dtype=jnp.int32)
    chosen = jnp.sum(
        jnp.where(
            route_rows[:, :, None] == expert_ids[None, None, :],
            logits[:, None, :],
            jnp.zeros((), logits.dtype),
        ),
        -1,
    )
    leading = jax.nn.sigmoid(chosen[:, 0] - chosen[:, 1])
    return jnp.stack([leading, 1.0 - leading], 1)


def slot_tables(route_rows, expert_count, capacity):
    token_count = route_rows.shape[0]
    expert_ids = jnp.arange(expert_count, dtype=jnp.int32)
    hits = (route_rows[:, :, None] == expert_ids[None, None, :]).astype(jnp.bfloat16)
    token_ids = jnp.arange(token_count)
    below = (token_ids[:, None] > token_ids[None, :]).astype(jnp.bfloat16)
    earlier = jnp.dot(below, hits.sum(1), preferred_element_type=jnp.float32)
    rank = jnp.sum(earlier[:, None, :] * hits.astype(jnp.float32), -1).astype(jnp.int32)
    slots = route_rows * capacity + rank
    slot_ids = jnp.arange(expert_count * capacity, dtype=jnp.int32)
    return slots[:, :, None] == slot_ids[None, None, :]


RINGS = (2, 4, 4)
SHARE = 512
BOTH = 1024
GROUP = 128
BLOCK = 256
TILE = 256


def shortest(offset):
    return sum(min(step, ring - step) for step, ring in zip(offset, RINGS))


OFFSETS = sorted(
    [(h, z, y) for h in range(RINGS[0]) for z in range(RINGS[1]) for y in range(RINGS[2])],
    key=shortest,
)


def expert_kernel(
    outgoing,
    first_hbm,
    second_hbm,
    returned,
    arrived,
    inner,
    first,
    second,
    for_partner,
    from_partner,
    both,
    share,
    load_sem,
    own_sem,
    send_sem,
    recv_sem,
    pass_sem,
    passed_sem,
    half_sem,
    halved_sem,
    back_sem,
    came_sem,
):
    row, mp = lax.axis_index("dp"), lax.axis_index("mp")
    cap = outgoing.shape[0] // len(OFFSETS)
    width = outgoing.shape[1]
    row_h, row_z, row_y = row // 16, row // 4 % 4, row % 4

    def place(offset, sign):
        dh, dz, dy = offset
        index = (
            (row_h + dh) % 2 * 16 + (row_z + sign * dz + 4) % 4 * 4 + (row_y + sign * dy + 4) % 4
        )
        return index, (mp + dh) % 2

    def device(index, side):
        return {"dp": index, "mp": side}

    partner = device(row, 1 - mp)
    barrier = pltpu.get_barrier_semaphore()
    for offset in OFFSETS[1:]:
        pl.semaphore_signal(barrier, inc=1, device_id=device(*place(offset, -1)), device_id_type=pl.DeviceIdType.MESH)
    pl.semaphore_signal(barrier, inc=1, device_id=partner, device_id_type=pl.DeviceIdType.MESH)

    loads = [
        pltpu.make_async_copy(first_hbm, first, load_sem.at[0]),
        pltpu.make_async_copy(second_hbm, second, load_sem.at[1]),
    ]
    for load in loads:
        load.start()
    pl.semaphore_wait(barrier, len(OFFSETS))

    def remote(source, target, sent, landed, where):
        return pltpu.make_async_remote_copy(
            source, target, sent, landed, device_id=where, device_id_type=pl.DeviceIdType.MESH
        )

    def dispatch(slot, side, index, where):
        columns = pl.ds(pl.multiple_of(side * SHARE, SHARE), SHARE + BOTH)
        source = outgoing.at[pl.ds(pl.multiple_of(index * cap, cap), cap), columns]
        target = arrived.at[pl.ds(slot * cap, cap), columns]
        if slot == 0:
            return pltpu.make_async_copy(source, target, own_sem.at[0])
        return remote(source, target, send_sem.at[slot], recv_sem.at[slot], where)

    sends = []
    for slot, offset in enumerate(OFFSETS):
        index, side = place(offset, 1)
        sends.append(dispatch(slot, side, index, device(index, side)))
        sends[slot].start()

    def wait_arrival(slot):
        if slot == 0:
            sends[0].wait()
        else:
            dispatch(slot, mp, row, partner).wait_recv()

    own_start = pl.multiple_of(mp * (SHARE + BOTH), SHARE)
    their_start = pl.multiple_of((1 - mp) * (SHARE + BOTH), SHARE)

    def forward(group, start):
        region = arrived.at[pl.ds(group * GROUP, GROUP), pl.ds(start, SHARE)]
        return remote(region, region, pass_sem.at[group], passed_sem.at[group], partner)

    def up_project(block):
        rows = pl.ds(block * BLOCK, BLOCK)

        def step(tile, carry):
            columns = pl.ds(pl.multiple_of(tile * TILE, TILE), TILE)
            product = jnp.dot(arrived[rows, :], first[:, columns], preferred_element_type=jnp.float32)
            inner[rows, columns] = jnp.maximum(product, 0.0).astype(jnp.bfloat16)
            return carry

        lax.fori_loop(0, inner.shape[1] // TILE, step, 0)

    groups = arrived.shape[0] // GROUP
    blocks = arrived.shape[0] // BLOCK
    per_group = GROUP // cap
    per_block = BLOCK // cap
    forwards = [forward(group, own_start) for group in range(groups)]
    for block in range(blocks + 1):
        if block < blocks:
            for group in range(block * BLOCK // GROUP, (block + 1) * BLOCK // GROUP):
                for slot in range(group * per_group, (group + 1) * per_group):
                    wait_arrival(slot)
                forwards[group].start()
        if block == 1:
            loads[0].wait()
        if block > 0:
            for group in range((block - 1) * BLOCK // GROUP, block * BLOCK // GROUP):
                forward(group, their_start).wait_recv()
            up_project(block - 1)

    def down_project(block, start, count, finish):
        rows = pl.ds(block * BLOCK, BLOCK)

        def step(tile, carry):
            columns = pl.ds(pl.multiple_of(start + tile * TILE, TILE), TILE)
            product = jnp.dot(inner[rows, :], second[:, columns], preferred_element_type=jnp.float32)
            finish(rows, pl.ds(pl.multiple_of(tile * TILE, TILE), TILE), product)
            return carry

        lax.fori_loop(0, count // TILE, step, 0)

    def keep_in(buffer):
        def finish(rows, columns, product):
            buffer[rows, columns] = product.astype(jnp.bfloat16)

        return finish

    def add_share(rows, columns, product):
        total = product + from_partner[rows, columns].astype(jnp.float32)
        share[rows, columns] = total.astype(jnp.bfloat16)

    def halve(block):
        rows = pl.ds(block * BLOCK, BLOCK)
        return remote(for_partner.at[rows], from_partner.at[rows], half_sem.at[block], halved_sem.at[block], partner)

    def give_back(slot, part, expert, where):
        buffer, start, count = ((both, 0, BOTH), (share, BOTH, SHARE))[part]
        source = buffer.at[pl.ds(slot * cap, cap)]
        target = returned.at[pl.ds(pl.multiple_of(expert * cap, cap), cap), pl.ds(start, count)]
        if slot == 0:
            return pltpu.make_async_copy(source, target, own_sem.at[1 + part])
        number = part * len(OFFSETS) + slot
        return remote(source, target, back_sem.at[number], came_sem.at[number], where)

    backs = []

    def give_block_back(block, part):
        for slot in range(block * per_block, (block + 1) * per_block):
            back = give_back(slot, part, row, device(*place(OFFSETS[slot], -1)))
            back.start()
            backs.append((slot, back))

    loads[1].wait()
    halves = [halve(block) for block in range(blocks)]
    for block in range(blocks):
        down_project(block, their_start, SHARE, keep_in(for_partner))
        halves[block].start()
    for block in range(blocks):
        down_project(block, SHARE, BOTH, keep_in(both))
        give_block_back(block, 0)
    for block in range(blocks):
        halves[block].wait_recv()
        down_project(block, own_start, SHARE, add_share)
        give_block_back(block, 1)

    for part in range(2):
        for slot in range(1, len(OFFSETS)):
            give_back(slot, part, place(OFFSETS[slot], 1)[0], partner).wait_recv()
    for slot, back in backs:
        if slot == 0:
            back.wait()
        else:
            back.wait_send()
    for slot in range(1, len(OFFSETS)):
        sends[slot].wait_send()
    for copy in forwards + halves:
        copy.wait_send()


def expert_exchange(outgoing, first, second):
    slots, width = outgoing.shape
    hidden = first.shape[1]
    count = len(OFFSETS)
    groups, blocks = slots // GROUP, slots // BLOCK
    dma = pltpu.SemaphoreType.DMA
    return pl.pallas_call(
        expert_kernel,
        out_shape=jax.ShapeDtypeStruct((slots, BOTH + SHARE), jnp.bfloat16),
        in_specs=[
            pl.BlockSpec(memory_space=pltpu.VMEM),
            pl.BlockSpec(memory_space=pl.ANY),
            pl.BlockSpec(memory_space=pl.ANY),
        ],
        out_specs=pl.BlockSpec(memory_space=pl.ANY),
        scratch_shapes=[
            pltpu.VMEM((slots, width), jnp.bfloat16),
            pltpu.VMEM((slots, hidden), jnp.bfloat16),
            pltpu.VMEM(first.shape, jnp.bfloat16),
            pltpu.VMEM(second.shape, jnp.bfloat16),
            pltpu.VMEM((slots, SHARE), jnp.bfloat16),
            pltpu.VMEM((slots, SHARE), jnp.bfloat16),
            pltpu.VMEM((slots, BOTH), jnp.bfloat16),
            pltpu.VMEM((slots, SHARE), jnp.bfloat16),
            dma((2,)),
            dma((3,)),
            dma((count,)),
            dma((count,)),
            dma((groups,)),
            dma((groups,)),
            dma((blocks,)),
            dma((blocks,)),
            dma((2 * count,)),
            dma((2 * count,)),
        ],
        compiler_params=pltpu.CompilerParams(
            collective_id=0, has_side_effects=True, vmem_limit_bytes=56 * 1024 * 1024
        ),
        cost_estimate=pl.CostEstimate(
            flops=4 * slots * width * hidden, bytes_accessed=24 * 1024 * 1024, transcendentals=0
        ),
        name="expert_exchange",
    )(outgoing, first, second)


def contract_rows(left_rows, weight):
    return lax.dot_general(
        left_rows, weight, (((1,), (1,)), ((), ())), preferred_element_type=jnp.float32
    )


def sum_rows(left, right):
    return lax.dot_general(left, right, (((0,), (0,)), ((), ())), preferred_element_type=jnp.float32)


def attend_head(query, key, value, grad, matches):
    softmax_scale = HEAD_DIM ** (-0.5)
    scores = contract_rows(query, key) * softmax_scale
    exp_scores = jnp.where(matches, jnp.exp(scores), 0.0)
    weights = exp_scores / jnp.sum(exp_scores, -1, keepdims=True)
    weights_b = weights.astype(jnp.bfloat16)
    context = jnp.dot(weights_b, value, preferred_element_type=jnp.float32)
    prob_grad = contract_rows(grad, value)
    row_delta = jnp.sum(weights * prob_grad, -1, keepdims=True)
    score_grad = (weights * (prob_grad - row_delta)).astype(jnp.bfloat16)
    query_grad = jnp.dot(score_grad, key, preferred_element_type=jnp.float32) * softmax_scale
    key_grad = sum_rows(score_grad, query) * softmax_scale
    value_grad = sum_rows(weights_b, grad)
    return [part.astype(jnp.bfloat16) for part in (key_grad, value_grad, query_grad, context)]


def layer_kernel(
    returned,
    coarse,
    fine,
    hidden,
    cotangent,
    weight_hbm,
    src_row,
    tgt_column,
    forward,
    backward,
    weight,
    mix_out,
    mix_in,
    own_mix,
    state,
    projected,
    held,
    grads,
    final_out,
    final_in,
    load_sem,
    mix_sent,
    mix_here,
    state_sent,
    state_here,
    held_sent,
    held_here,
    grad_sent,
    grad_here,
    final_sent,
    final_here,
):
    group, row, mp = lax.axis_index("grp"), lax.axis_index("dp"), lax.axis_index("mp")
    partner, core = {"mp": 1 - mp}, {"grp": 1 - group}
    barrier = pltpu.get_barrier_semaphore()
    for where in (partner, core):
        pl.semaphore_signal(barrier, inc=1, device_id=where, device_id_type=pl.DeviceIdType.MESH)
    load = pltpu.make_async_copy(weight_hbm, weight, load_sem.at[0])
    load.start()

    def remote(source, target, sent, landed, where):
        return pltpu.make_async_remote_copy(
            source, target, sent, landed, device_id=where, device_id_type=pl.DeviceIdType.MESH
        )

    half = BOTH
    my_side = row // 16
    slots = returned.shape[0]

    def span(start, count=SHARE):
        return pl.ds(pl.multiple_of(start, SHARE), count)

    def mix_rows(rows, columns):
        values = returned[rows, columns]
        return jnp.dot(coarse[:, rows], values, preferred_element_type=jnp.float32) + jnp.dot(
            fine[:, rows], values, preferred_element_type=jnp.float32
        )

    def mix_part(part, side):
        if part == 0:
            return mix_rows(pl.ds(0, slots), span(side * SHARE))
        which = (my_side + (side - mp) * (side - mp)) % 2
        return mix_rows(span(which * (slots // 2), slots // 2), pl.ds(BOTH, SHARE))

    def piece(part, side):
        return span(SHARE + side * SHARE) if part == 0 else span(side * (SHARE + BOTH))

    mixes = [
        remote(mix_out.at[part], mix_in.at[part], mix_sent.at[part], mix_here.at[part], partner)
        for part in range(2)
    ]
    pl.semaphore_wait(barrier, 2)
    for part in range(2):
        mix_out[part] = mix_part(part, 1 - mp).astype(jnp.bfloat16)
        mixes[part].start()
    for part in range(2):
        own_mix[part] = mix_part(part, mp)

    def project(source, which, columns):
        return jnp.dot(source[:, columns], weight[which, columns, :], preferred_element_type=jnp.float32)

    load.wait()

    @pl.when(group == 1)
    def _():
        projected[1] = project(cotangent, 1, pl.ds(0, 2 * half))

    def hand_state(part, side):
        region = state.at[:, piece(part, side)]
        return remote(region, region, state_sent.at[part], state_here.at[part], partner)

    hands = [hand_state(part, mp) for part in range(2)]
    for part in range(2):
        mixes[part].wait_recv()
        columns = piece(part, mp)
        total = hidden[:, columns].astype(jnp.float32) + (
            own_mix[part] + mix_in[part].astype(jnp.float32)
        )
        state[:, columns] = total.astype(jnp.bfloat16)
        hands[part].start()

    order = [(0, mp), (1, mp), (0, 1 - mp), (1, 1 - mp)]
    for number, (part, side) in enumerate(order):
        if number >= 2:
            hand_state(part, side).wait_recv()
        columns = piece(part, side)
        term = project(state, 0, columns)
        projected[0] = term if number == 0 else projected[0] + term

        @pl.when(group == 0)
        def _():
            other = project(state, 1, columns)
            projected[1] = other if number == 0 else projected[1] + other

    pair = 2 * HEAD_DIM
    for which in range(2):
        for heads in range(2):
            held[group, which, heads] = projected[which, :, heads * pair : (heads + 1) * pair].astype(
                jnp.bfloat16
            )

    def hand_held(which, owner, heads):
        region = held.at[owner, which, heads]
        return remote(region, region, held_sent.at[which], held_here.at[which], core)

    handed = [hand_held(which, group, 1 - group) for which in range(2)]
    for which in range(2):
        handed[which].start()
    matches = tgt_column[...] == src_row[...]
    for which in range(2):
        hand_held(which, 1 - group, group).wait_recv()

    for head in range(2):
        columns = slice(head * HEAD_DIM, (head + 1) * HEAD_DIM)
        results = attend_head(
            held[1, 0, group][:, columns],
            held[0, 0, group][:, columns],
            held[0, 1, group][:, columns],
            held[1, 1, group][:, columns],
            matches,
        )
        for number, result in enumerate(results):
            grads[number // 2, number % 2, group, :, columns] = result

    def hand_grad(which, owner, heads):
        region = grads.at[owner, which, heads]
        return remote(region, region, grad_sent.at[which], grad_here.at[which], core)

    given = [hand_grad(which, 1 - group, group) for which in range(2)]
    for which in range(2):
        given[which].start()
    for which in range(2):
        hand_grad(which, group, 1 - group).wait_recv()

    def back_project(which, start):
        rows = span(start)
        return contract_rows(grads[group, which, 0], weight[which, rows, :pair]) + contract_rows(
            grads[group, which, 1], weight[which, rows, pair:]
        )

    def final(which, chunk):
        number = which * 2 + chunk
        return remote(
            final_out.at[number], final_in.at[number], final_sent.at[number], final_here.at[number], partner
        )

    @pl.when(group == 0)
    def _():
        for chunk in range(2):
            start = (1 - mp) * half + chunk * SHARE
            final_out[chunk] = (back_project(0, start) + back_project(1, start)).astype(jnp.bfloat16)
            final(0, chunk).start()
        forward[...] = state[:, span(mp * half, half)]
        for chunk in range(2):
            start = mp * half + chunk * SHARE
            own = back_project(0, start) + back_project(1, start)
            final(0, chunk).wait_recv()
            backward[:, chunk * SHARE : (chunk + 1) * SHARE] = (
                own + final_in[chunk].astype(jnp.float32)
            ).astype(jnp.bfloat16)
        for chunk in range(2):
            final(0, chunk).wait_send()

    @pl.when(group == 1)
    def _():
        for which in range(2):
            for chunk in range(2):
                start = (1 - mp) * half + chunk * SHARE
                final_out[which * 2 + chunk] = back_project(which, start).astype(jnp.bfloat16)
                final(which, chunk).start()
        for which, base, target in ((0, cotangent, backward), (1, state, forward)):
            for chunk in range(2):
                start = mp * half + chunk * SHARE
                own = back_project(which, start)
                final(which, chunk).wait_recv()
                total = base[:, span(start)].astype(jnp.float32) + (
                    own + final_in[which * 2 + chunk].astype(jnp.float32)
                )
                target[:, chunk * SHARE : (chunk + 1) * SHARE] = total.astype(jnp.bfloat16)
        for which in range(2):
            for chunk in range(2):
                final(which, chunk).wait_send()

    for copy in mixes + hands + handed + given:
        copy.wait_send()


def finish_layer(returned, coarse, fine, hidden, cotangent, weight, src_row, tgt_column):
    tokens, width = hidden.shape
    half = width // 2
    dma = pltpu.SemaphoreType.DMA
    vmem = pl.BlockSpec(memory_space=pltpu.VMEM)
    pair = 2 * HEAD_DIM
    return pl.pallas_call(
        layer_kernel,
        out_shape=[jax.ShapeDtypeStruct((tokens, half), jnp.bfloat16)] * 2,
        in_specs=[vmem] * 5 + [pl.BlockSpec(memory_space=pl.ANY)] + [vmem] * 2,
        out_specs=[vmem] * 2,
        scratch_shapes=[
            pltpu.VMEM(weight.shape, jnp.bfloat16),
            pltpu.VMEM((2, tokens, SHARE), jnp.bfloat16),
            pltpu.VMEM((2, tokens, SHARE), jnp.bfloat16),
            pltpu.VMEM((2, tokens, SHARE), jnp.float32),
            pltpu.VMEM((tokens, width), jnp.bfloat16),
            pltpu.VMEM((2, tokens, 2 * pair), jnp.float32),
            pltpu.VMEM((2, 2, 2, tokens, pair), jnp.bfloat16),
            pltpu.VMEM((2, 2, 2, tokens, pair), jnp.bfloat16),
            pltpu.VMEM((4, tokens, SHARE), jnp.bfloat16),
            pltpu.VMEM((4, tokens, SHARE), jnp.bfloat16),
            dma((1,)),
        ]
        + [dma((2,))] * 8
        + [dma((4,))] * 2,
        compiler_params=pltpu.CompilerParams(
            collective_id=1, has_side_effects=True, vmem_limit_bytes=48 * 1024 * 1024
        ),
        cost_estimate=pl.CostEstimate(
            flops=12 * tokens * width * half, bytes_accessed=12 * 1024 * 1024, transcendentals=131072
        ),
        name="finish_layer",
    )(returned, coarse, fine, hidden, cotangent, weight, src_row, tgt_column)


def per_device(
    hidden_in,
    norm_gain,
    router,
    routes,
    expert_in,
    expert_out,
    attn_weight,
    src_segments,
    tgt_segments,
    cotangent,
):
    expert_count = lax.axis_size("dp")
    token_rows = hidden_in[0]
    token_count, model_width = token_rows.shape
    capacity = 4 * token_count // expert_count
    normed = layer_norm(token_rows, norm_gain[0])
    route_rows = routes[0]
    gate_rows = gate_pairs(normed, router[0], route_rows)
    places = slot_tables(route_rows, expert_count, capacity)
    weight_in = expert_in[0, 0]
    weight_out = expert_out[0, 0]
    outgoing = lax.dot_general(
        places.any(1).astype(jnp.bfloat16),
        normed,
        (((0,), (0,)), ((), ())),
        preferred_element_type=jnp.float32,
    ).astype(jnp.bfloat16)
    returned = expert_exchange(outgoing, weight_in, weight_out)
    mixing = jnp.sum(jnp.where(places, gate_rows[:, :, None], 0.0), 1)
    coarse = mixing.astype(jnp.bfloat16)
    fine = (mixing - coarse.astype(jnp.float32)).astype(jnp.bfloat16)
    forward, backward = finish_layer(
        returned,
        coarse,
        fine,
        token_rows,
        cotangent,
        attn_weight[0],
        src_segments,
        tgt_segments.reshape(token_count, 1),
    )
    return (forward[None], backward[None])


def solution(mesh):
    return jax.shard_map(
        per_device,
        mesh=mesh,
        in_specs=(
            P("grp", "dp", None),
            P("grp", None),
            P("grp", None, None),
            P("grp", "dp", None),
            P("grp", "dp", None, "mp"),
            P("grp", "dp", "mp", None),
            P("grp", None, None, "mp"),
            P("dp", None),
            P("dp", None),
            P("dp", None),
        ),
        out_specs=(P("grp", "dp", "mp"), P("grp", "dp", "mp")),
        check_vma=False,
    )
```

```python
import jax
import jax.numpy as jnp
from jax import lax
from jax.experimental import pallas as pl
from jax.experimental.pallas import tpu as pltpu
from jax.sharding import PartitionSpec as P

HEAD_DIM = 128


RINGS = (2, 4, 4)
SHARE = 512
BOTH = 1024
GROUP = 128
BLOCK = 256
TILE = 256


def shortest(offset):
    return sum(min(step, ring - step) for step, ring in zip(offset, RINGS))


OFFSETS = sorted(
    [(h, z, y) for h in range(RINGS[0]) for z in range(RINGS[1]) for y in range(RINGS[2])],
    key=shortest,
)


def contract_rows(left_rows, weight):
    return lax.dot_general(
        left_rows, weight, (((1,), (1,)), ((), ())), preferred_element_type=jnp.float32
    )


def sum_rows(left, right):
    return lax.dot_general(left, right, (((0,), (0,)), ((), ())), preferred_element_type=jnp.float32)


def attend_head(query, key, value, grad, matches):
    softmax_scale = HEAD_DIM ** (-0.5)
    scores = contract_rows(query, key) * softmax_scale
    exp_scores = jnp.where(matches, jnp.exp(scores), 0.0)
    weights = exp_scores / jnp.sum(exp_scores, -1, keepdims=True)
    weights_b = weights.astype(jnp.bfloat16)
    context = jnp.dot(weights_b, value, preferred_element_type=jnp.float32)
    prob_grad = contract_rows(grad, value)
    row_delta = jnp.sum(weights * prob_grad, -1, keepdims=True)
    score_grad = (weights * (prob_grad - row_delta)).astype(jnp.bfloat16)
    query_grad = jnp.dot(score_grad, key, preferred_element_type=jnp.float32) * softmax_scale
    key_grad = sum_rows(score_grad, query) * softmax_scale
    value_grad = sum_rows(weights_b, grad)
    return [part.astype(jnp.bfloat16) for part in (key_grad, value_grad, query_grad, context)]


def layer_kernel(
    hidden,
    gain,
    router,
    routes,
    routes_t,
    src_row,
    tgt_column,
    first_hbm,
    second_hbm,
    weight_hbm,
    cotangent_hbm,
    forward,
    backward,
    normed,
    outgoing,
    arrived,
    inner,
    first,
    second,
    weight,
    cotangent,
    coarse,
    fine,
    for_partner,
    from_partner,
    both,
    share,
    returned,
    mix_out,
    mix_in,
    own_mix,
    state,
    projected,
    held,
    grads,
    final_out,
    final_in,
    load_sem,
    own_sem,
    send_sem,
    recv_sem,
    pass_sem,
    passed_sem,
    half_sem,
    halved_sem,
    back_sem,
    came_sem,
    mix_sent,
    mix_here,
    state_sent,
    state_here,
    held_sent,
    held_here,
    grad_sent,
    grad_here,
    final_sent,
    final_here,
):
    group, row, mp = lax.axis_index("grp"), lax.axis_index("dp"), lax.axis_index("mp")
    experts = len(OFFSETS)
    slots, width = outgoing.shape
    tokens = hidden.shape[0]
    cap = slots // experts
    half = width // 2
    row_h, row_z, row_y = row // 16, row // 4 % 4, row % 4
    partner, core = {"mp": 1 - mp}, {"grp": 1 - group}

    def place(offset, sign):
        dh, dz, dy = offset
        index = (
            (row_h + dh) % 2 * 16 + (row_z + sign * dz + 4) % 4 * 4 + (row_y + sign * dy + 4) % 4
        )
        return index, (mp + dh) % 2

    def device(index, side):
        return {"dp": index, "mp": side}

    def remote(source, target, sent, landed, where):
        return pltpu.make_async_remote_copy(
            source, target, sent, landed, device_id=where, device_id_type=pl.DeviceIdType.MESH
        )

    def span(start, count=SHARE):
        return pl.ds(pl.multiple_of(start, SHARE), count)

    barrier = pltpu.get_barrier_semaphore()
    greeted = [device(*place(offset, -1)) for offset in OFFSETS[1:]] + [partner, core]
    for where in greeted:
        pl.semaphore_signal(barrier, inc=1, device_id=where, device_id_type=pl.DeviceIdType.MESH)
    loads = [
        pltpu.make_async_copy(source, target, load_sem.at[number])
        for number, (source, target) in enumerate(
            ((first_hbm, first), (weight_hbm, weight), (cotangent_hbm, cotangent), (second_hbm, second))
        )
    ]
    for load in loads:
        load.start()

    norm_rows = 64

    def normalise(step, carry):
        rows = pl.ds(pl.multiple_of(step * norm_rows, norm_rows), norm_rows)
        values = hidden[rows, :].astype(jnp.float32)
        centred = values - jnp.mean(values, -1, keepdims=True)
        variance = jnp.mean(centred * centred, -1, keepdims=True)
        scaled = centred * lax.rsqrt(variance + 1e-05) * gain[...].astype(jnp.float32)
        normed[rows, :] = scaled.astype(jnp.bfloat16)
        return carry

    lax.fori_loop(0, tokens // norm_rows, normalise, 0)

    def iota(shape, axis):
        return lax.broadcasted_iota(jnp.int32, shape, axis)

    def ones_where(mask):
        return jnp.where(mask, 1.0, 0.0)

    square = (tokens, tokens)
    named_t = [routes_t[k : k + 1, :] == iota((experts, tokens), 0) for k in range(2)]
    earlier_t = jnp.dot(
        (ones_where(named_t[0]) + ones_where(named_t[1])).astype(jnp.bfloat16),
        ones_where(iota(square, 0) < iota(square, 1)).astype(jnp.bfloat16),
        preferred_element_type=jnp.float32,
    )
    rank_t = [jnp.sum(jnp.where(mask, earlier_t, 0.0), 0, keepdims=True) for mask in named_t]
    places = iota((cap, tokens), 0).astype(jnp.float32)

    def slot_rows(slot):
        expert = place(OFFSETS[slot], 1)[0]
        rank = jnp.where(
            routes_t[0:1, :] == expert, rank_t[0], jnp.where(routes_t[1:2, :] == expert, rank_t[1], -1.0)
        )
        return ones_where(rank == places)

    def dispatch(slot, part, side, where):
        columns = span(side * (SHARE + BOTH)) if part == 0 else pl.ds(SHARE, BOTH)
        source = outgoing.at[pl.ds(slot * cap, cap), columns]
        target = arrived.at[pl.ds(slot * cap, cap), columns]
        if slot == 0:
            return pltpu.make_async_copy(source, target, own_sem.at[part])
        number = part * experts + slot
        return remote(source, target, send_sem.at[number], recv_sem.at[number], where)

    sends = []

    def send(slot, part):
        index, side = place(OFFSETS[slot], 1)
        sends.append((slot, part, dispatch(slot, part, side, device(index, side))))
        sends[-1][2].start()

    blocks = slots // BLOCK
    per_block = BLOCK // cap
    for block in range(blocks):
        chosen = jnp.concatenate(
            [slot_rows(slot) for slot in range(block * per_block, (block + 1) * per_block)], 0
        ).astype(jnp.bfloat16)
        for start in range(0, width, SHARE):
            outgoing[block * BLOCK : (block + 1) * BLOCK, start : start + SHARE] = jnp.dot(
                chosen, normed[:, start : start + SHARE], preferred_element_type=jnp.float32
            ).astype(jnp.bfloat16)
        if block == 0:
            pl.semaphore_wait(barrier, len(greeted))
        for slot in range(block * per_block, (block + 1) * per_block):
            send(slot, 0)
    for slot in range(experts):
        send(slot, 1)

    named = [routes[:, k : k + 1] == iota((tokens, experts), 1) for k in range(2)]
    earlier = jnp.dot(
        ones_where(iota(square, 0) > iota(square, 1)).astype(jnp.bfloat16),
        (ones_where(named[0]) + ones_where(named[1])).astype(jnp.bfloat16),
        preferred_element_type=jnp.float32,
    )
    logits = jnp.dot(normed[...], router[...], preferred_element_type=jnp.float32)

    def chosen_of(values, k):
        return jnp.sum(jnp.where(named[k], values, 0.0), 1, keepdims=True)

    leading = jax.nn.sigmoid(chosen_of(logits, 0) - chosen_of(logits, 1))
    gates = (leading, 1.0 - leading)
    spots = [routes[:, k : k + 1] * cap + chosen_of(earlier, k).astype(jnp.int32) for k in range(2)]
    for start in range(0, slots, BLOCK):
        columns = iota((tokens, BLOCK), 1) + start
        mixing = jnp.where(spots[0] == columns, gates[0], 0.0) + jnp.where(spots[1] == columns, gates[1], 0.0)
        rough = mixing.astype(jnp.bfloat16)
        coarse[:, start : start + BLOCK] = rough
        fine[:, start : start + BLOCK] = (mixing - rough.astype(jnp.float32)).astype(jnp.bfloat16)

    def wait_arrival(slot, part):
        if slot == 0:
            sends[0 if part == 0 else experts][2].wait()
        else:
            dispatch(slot, part, mp, partner).wait_recv()

    own_start = mp * (SHARE + BOTH)
    their_start = (1 - mp) * (SHARE + BOTH)

    def pass_on(number, start):
        region = arrived.at[pl.ds(number * GROUP, GROUP), span(start)]
        return remote(region, region, pass_sem.at[number], passed_sem.at[number], partner)

    groups = slots // GROUP
    per_group = GROUP // cap
    passes = [pass_on(number, own_start) for number in range(groups)]
    for number in range(groups):
        for slot in range(number * per_group, (number + 1) * per_group):
            wait_arrival(slot, 0)
        passes[number].start()

    def project(source, which, columns):
        return jnp.dot(source[:, columns], weight[which, columns, :], preferred_element_type=jnp.float32)

    for load in loads[:3]:
        load.wait()

    @pl.when(group == 1)
    def _():
        projected[1] = project(cotangent, 1, pl.ds(0, width))

    def up_project(block):
        rows = pl.ds(block * BLOCK, BLOCK)

        def step(tile, carry):
            columns = pl.ds(pl.multiple_of(tile * TILE, TILE), TILE)
            product = jnp.dot(arrived[rows, :], first[:, columns], preferred_element_type=jnp.float32)
            inner[rows, columns] = jnp.maximum(product, 0.0).astype(jnp.bfloat16)
            return carry

        lax.fori_loop(0, inner.shape[1] // TILE, step, 0)

    for block in range(blocks):
        for number in range(block * BLOCK // GROUP, (block + 1) * BLOCK // GROUP):
            pass_on(number, their_start).wait_recv()
        for slot in range(block * per_block, (block + 1) * per_block):
            wait_arrival(slot, 1)
        up_project(block)

    def down_project(block, start, count, finish):
        rows = pl.ds(block * BLOCK, BLOCK)

        def step(tile, carry):
            columns = pl.ds(pl.multiple_of(start + tile * TILE, TILE), TILE)
            product = jnp.dot(inner[rows, :], second[:, columns], preferred_element_type=jnp.float32)
            finish(rows, pl.ds(pl.multiple_of(tile * TILE, TILE), TILE), product)
            return carry

        lax.fori_loop(0, count // TILE, step, 0)

    def keep_in(buffer):
        def finish(rows, columns, product):
            buffer[rows, columns] = product.astype(jnp.bfloat16)

        return finish

    def add_share(rows, columns, product):
        total = product + from_partner[rows, columns].astype(jnp.float32)
        share[rows, columns] = total.astype(jnp.bfloat16)

    def halve(block):
        rows = pl.ds(block * BLOCK, BLOCK)
        return remote(for_partner.at[rows], from_partner.at[rows], half_sem.at[block], halved_sem.at[block], partner)

    def give_back(slot, part, expert, where):
        buffer, start, count = ((both, 0, BOTH), (share, BOTH, SHARE))[part]
        source = buffer.at[pl.ds(slot * cap, cap)]
        target = returned.at[pl.ds(pl.multiple_of(expert * cap, cap), cap), pl.ds(start, count)]
        if slot == 0:
            return pltpu.make_async_copy(source, target, own_sem.at[2 + part])
        number = part * experts + slot
        return remote(source, target, back_sem.at[number], came_sem.at[number], where)

    backs = []

    def give_block_back(block, part):
        for slot in range(block * per_block, (block + 1) * per_block):
            backs.append((slot, part, give_back(slot, part, row, device(*place(OFFSETS[slot], -1)))))
            backs[-1][2].start()

    loads[3].wait()
    halves = [halve(block) for block in range(blocks)]
    for block in range(blocks):
        down_project(block, their_start, SHARE, keep_in(for_partner))
        halves[block].start()
    for block in range(blocks):
        down_project(block, SHARE, BOTH, keep_in(both))
        give_block_back(block, 0)
    for block in range(blocks):
        halves[block].wait_recv()
        down_project(block, own_start, SHARE, add_share)
        give_block_back(block, 1)

    def mix_rows(rows, columns):
        values = returned[rows, columns]
        return jnp.dot(coarse[:, rows], values, preferred_element_type=jnp.float32) + jnp.dot(
            fine[:, rows], values, preferred_element_type=jnp.float32
        )

    def mix_part(part, mine):
        if part == 0:
            return mix_rows(pl.ds(0, slots), span((mp if mine else 1 - mp) * SHARE))
        which = row_h if mine else 1 - row_h
        return mix_rows(span(which * (slots // 2), slots // 2), pl.ds(BOTH, SHARE))

    def piece(part, side):
        return span(SHARE + side * SHARE) if part == 0 else span(side * (SHARE + BOTH))

    mixes = [
        remote(mix_out.at[part], mix_in.at[part], mix_sent.at[part], mix_here.at[part], partner)
        for part in range(2)
    ]

    def hand_state(part, side):
        region = state.at[:, piece(part, side)]
        return remote(region, region, state_sent.at[part], state_here.at[part], partner)

    hands = [hand_state(part, mp) for part in range(2)]

    def project_piece(part, side, opening):
        columns = piece(part, side)
        term = project(state, 0, columns)
        projected[0] = term if opening else projected[0] + term

        @pl.when(group == 0)
        def _():
            other = project(state, 1, columns)
            projected[1] = other if opening else projected[1] + other

    for part in range(2):
        for slot in range(experts):
            if slot > 0:
                give_back(slot, part, place(OFFSETS[slot], 1)[0], partner).wait_recv()
            else:
                backs[part * experts][2].wait()
        mix_out[part] = mix_part(part, False).astype(jnp.bfloat16)
        mixes[part].start()
        own_mix[part] = mix_part(part, True)
        mixes[part].wait_recv()
        columns = piece(part, mp)
        total = hidden[:, columns].astype(jnp.float32) + (
            own_mix[part] + mix_in[part].astype(jnp.float32)
        )
        state[:, columns] = total.astype(jnp.bfloat16)
        hands[part].start()
        project_piece(part, mp, part == 0)
    for part in range(2):
        hand_state(part, 1 - mp).wait_recv()
        project_piece(part, 1 - mp, False)

    pair = 2 * HEAD_DIM
    for which in range(2):
        for heads in range(2):
            held[group, which, heads] = projected[which, :, heads * pair : (heads + 1) * pair].astype(
                jnp.bfloat16
            )

    def hand_held(which, owner, heads):
        region = held.at[owner, which, heads]
        return remote(region, region, held_sent.at[which], held_here.at[which], core)

    handed = [hand_held(which, group, 1 - group) for which in range(2)]
    for which in range(2):
        handed[which].start()
    matches = tgt_column[...] == src_row[...]
    for which in range(2):
        hand_held(which, 1 - group, group).wait_recv()

    for head in range(2):
        columns = slice(head * HEAD_DIM, (head + 1) * HEAD_DIM)
        results = attend_head(
            held[1, 0, group][:, columns],
            held[0, 0, group][:, columns],
            held[0, 1, group][:, columns],
            held[1, 1, group][:, columns],
            matches,
        )
        for number, result in enumerate(results):
            grads[number // 2, number % 2, group, :, columns] = result

    def hand_grad(which, owner, heads):
        region = grads.at[owner, which, heads]
        return remote(region, region, grad_sent.at[which], grad_here.at[which], core)

    given = [hand_grad(which, 1 - group, group) for which in range(2)]
    for which in range(2):
        given[which].start()
    for which in range(2):
        hand_grad(which, group, 1 - group).wait_recv()

    def back_project(which, start):
        rows = span(start)
        return contract_rows(grads[group, which, 0], weight[which, rows, :pair]) + contract_rows(
            grads[group, which, 1], weight[which, rows, pair:]
        )

    def final(which, chunk):
        number = which * 2 + chunk
        return remote(
            final_out.at[number], final_in.at[number], final_sent.at[number], final_here.at[number], partner
        )

    @pl.when(group == 0)
    def _():
        for chunk in range(2):
            start = (1 - mp) * half + chunk * SHARE
            final_out[chunk] = (back_project(0, start) + back_project(1, start)).astype(jnp.bfloat16)
            final(0, chunk).start()
        forward[...] = state[:, span(mp * half, half)]
        for chunk in range(2):
            start = mp * half + chunk * SHARE
            own = back_project(0, start) + back_project(1, start)
            final(0, chunk).wait_recv()
            backward[:, chunk * SHARE : (chunk + 1) * SHARE] = (
                own + final_in[chunk].astype(jnp.float32)
            ).astype(jnp.bfloat16)
        for chunk in range(2):
            final(0, chunk).wait_send()

    @pl.when(group == 1)
    def _():
        for which in range(2):
            for chunk in range(2):
                start = (1 - mp) * half + chunk * SHARE
                final_out[which * 2 + chunk] = back_project(which, start).astype(jnp.bfloat16)
                final(which, chunk).start()
        for which, base, target in ((0, cotangent, backward), (1, state, forward)):
            for chunk in range(2):
                start = mp * half + chunk * SHARE
                own = back_project(which, start)
                final(which, chunk).wait_recv()
                total = base[:, span(start)].astype(jnp.float32) + (
                    own + final_in[which * 2 + chunk].astype(jnp.float32)
                )
                target[:, chunk * SHARE : (chunk + 1) * SHARE] = total.astype(jnp.bfloat16)
        for which in range(2):
            for chunk in range(2):
                final(which, chunk).wait_send()

    for slot, part, copy in sends + backs:
        if slot > 0:
            copy.wait_send()
    for copy in passes + halves + mixes + hands + handed + given:
        copy.wait_send()


def whole_layer(hidden, gain, router, routes, src_row, tgt_column, first, second, weight, cotangent):
    tokens, width = hidden.shape
    half, inner = width // 2, first.shape[1]
    experts = router.shape[1]
    slots = 4 * tokens
    pair = 2 * HEAD_DIM
    dma = pltpu.SemaphoreType.DMA
    vmem = pl.BlockSpec(memory_space=pltpu.VMEM)
    shapes = [
        (tokens, width),
        (slots, width),
        (slots, width),
        (slots, inner),
        first.shape,
        second.shape,
        weight.shape,
        cotangent.shape,
        (tokens, slots),
        (tokens, slots),
        (slots, SHARE),
        (slots, SHARE),
        (slots, BOTH),
        (slots, SHARE),
        (slots, BOTH + SHARE),
        (2, tokens, SHARE),
        (2, tokens, SHARE),
        None,
        (tokens, width),
        None,
        (2, 2, 2, tokens, pair),
        (2, 2, 2, tokens, pair),
        (4, tokens, SHARE),
        (4, tokens, SHARE),
    ]
    scratch = [
        pltpu.VMEM((2, tokens, SHARE), jnp.float32) if shape is None else pltpu.VMEM(shape, jnp.bfloat16)
        for shape in shapes
    ]
    counts = [4, 4] + [2 * experts] * 2 + [slots // GROUP] * 2 + [slots // BLOCK] * 2 + [2 * experts] * 2
    counts += [2] * 8 + [4] * 2
    return pl.pallas_call(
        layer_kernel,
        out_shape=[jax.ShapeDtypeStruct((tokens, half), jnp.bfloat16)] * 2,
        in_specs=[vmem] * 7 + [pl.BlockSpec(memory_space=pl.ANY)] * 4,
        out_specs=[vmem] * 2,
        scratch_shapes=scratch + [dma((count,)) for count in counts],
        compiler_params=pltpu.CompilerParams(
            collective_id=0, has_side_effects=True, vmem_limit_bytes=60 * 1024 * 1024
        ),
        cost_estimate=pl.CostEstimate(
            flops=4 * slots * width * inner, bytes_accessed=24 * 1024 * 1024, transcendentals=131072
        ),
        name="whole_layer",
    )(
        hidden,
        gain,
        router,
        routes,
        routes.T,
        src_row,
        tgt_column,
        first,
        second,
        weight,
        cotangent,
    )


def per_device(
    hidden_in,
    norm_gain,
    router,
    routes,
    expert_in,
    expert_out,
    attn_weight,
    src_segments,
    tgt_segments,
    cotangent,
):
    forward, backward = whole_layer(
        hidden_in[0],
        norm_gain,
        router[0],
        routes[0],
        src_segments,
        tgt_segments.reshape(-1, 1),
        expert_in[0, 0],
        expert_out[0, 0],
        attn_weight[0],
        cotangent,
    )
    return (forward[None], backward[None])


def solution(mesh):
    return jax.shard_map(
        per_device,
        mesh=mesh,
        in_specs=(
            P("grp", "dp", None),
            P("grp", None),
            P("grp", None, None),
            P("grp", "dp", None),
            P("grp", "dp", None, "mp"),
            P("grp", "dp", "mp", None),
            P("grp", None, None, "mp"),
            P("dp", None),
            P("dp", None),
            P("dp", None),
        ),
        out_specs=(P("grp", "dp", "mp"), P("grp", "dp", "mp")),
        check_vma=False,
    )
```

```python
import jax
import jax.numpy as jnp
from jax import lax
from jax.experimental import pallas as pl
from jax.experimental.pallas import tpu as pltpu
from jax.sharding import PartitionSpec as P

HEAD_DIM = 128


RINGS = (2, 4, 4)
SHARE = 512
BOTH = 1024
LATE = 256
GROUP = 128
BLOCK = 256
TILE = 256


def shortest(offset):
    return sum(min(step, ring - step) for step, ring in zip(offset, RINGS))


OFFSETS = sorted(
    [(h, z, y) for h in range(RINGS[0]) for z in range(RINGS[1]) for y in range(RINGS[2])],
    key=shortest,
)


def contract_rows(left_rows, weight):
    return lax.dot_general(
        left_rows, weight, (((1,), (1,)), ((), ())), preferred_element_type=jnp.float32
    )


def sum_rows(left, right):
    return lax.dot_general(left, right, (((0,), (0,)), ((), ())), preferred_element_type=jnp.float32)


def attend_head(query, key, value, grad, matches):
    softmax_scale = HEAD_DIM ** (-0.5)
    scores = contract_rows(query, key) * softmax_scale
    exp_scores = jnp.where(matches, jnp.exp(scores), 0.0)
    weights = exp_scores / jnp.sum(exp_scores, -1, keepdims=True)
    weights_b = weights.astype(jnp.bfloat16)
    context = jnp.dot(weights_b, value, preferred_element_type=jnp.float32)
    prob_grad = contract_rows(grad, value)
    row_delta = jnp.sum(weights * prob_grad, -1, keepdims=True)
    score_grad = (weights * (prob_grad - row_delta)).astype(jnp.bfloat16)
    query_grad = jnp.dot(score_grad, key, preferred_element_type=jnp.float32) * softmax_scale
    key_grad = sum_rows(score_grad, query) * softmax_scale
    value_grad = sum_rows(weights_b, grad)
    return [part.astype(jnp.bfloat16) for part in (key_grad, value_grad, query_grad, context)]


def layer_kernel(
    hidden,
    gain,
    router_t,
    routes_t,
    src_row,
    tgt_row,
    first_hbm,
    second_hbm,
    weight_hbm,
    cotangent_hbm,
    forward,
    backward,
    normed,
    outgoing,
    arrived,
    inner,
    first,
    second,
    weight,
    cotangent,
    coarse,
    fine,
    match_rows,
    for_partner,
    from_partner,
    both,
    share,
    returned,
    mix_out,
    mix_in,
    state,
    projected,
    held,
    grads,
    final_out,
    final_in,
    load_sem,
    own_sem,
    send_sem,
    recv_sem,
    pass_sem,
    passed_sem,
    half_sem,
    halved_sem,
    back_sem,
    came_sem,
    mix_sent,
    mix_here,
    state_sent,
    state_here,
    held_sent,
    held_here,
    grad_sent,
    grad_here,
    final_sent,
    final_here,
):
    group, row, mp = lax.axis_index("grp"), lax.axis_index("dp"), lax.axis_index("mp")
    experts = len(OFFSETS)
    slots, width = outgoing.shape
    tokens = hidden.shape[0]
    cap = slots // experts
    half = width // 2
    row_h, row_z, row_y = row // 16, row // 4 % 4, row % 4
    partner, core = {"mp": 1 - mp}, {"grp": 1 - group}

    def place(offset, sign):
        dh, dz, dy = offset
        index = (
            (row_h + dh) % 2 * 16 + (row_z + sign * dz + 4) % 4 * 4 + (row_y + sign * dy + 4) % 4
        )
        return index, (mp + dh) % 2

    def device(index, side):
        return {"dp": index, "mp": side}

    def remote(source, target, sent, landed, where):
        return pltpu.make_async_remote_copy(
            source, target, sent, landed, device_id=where, device_id_type=pl.DeviceIdType.MESH
        )

    def span(start, count=SHARE):
        return pl.ds(pl.multiple_of(start, SHARE), count)

    barrier = pltpu.get_barrier_semaphore()
    greeted = [device(*place(offset, -1)) for offset in OFFSETS[1:]] + [partner, core]
    for where in greeted:
        pl.semaphore_signal(barrier, inc=1, device_id=where, device_id_type=pl.DeviceIdType.MESH)
    loads = [
        pltpu.make_async_copy(source, target, load_sem.at[number])
        for number, (source, target) in enumerate(
            ((first_hbm, first), (weight_hbm, weight), (cotangent_hbm, cotangent), (second_hbm, second))
        )
    ]
    for load in loads:
        load.start()

    norm_rows = 64

    def normalise(step, carry):
        rows = pl.ds(pl.multiple_of(step * norm_rows, norm_rows), norm_rows)
        values = hidden[rows, :].astype(jnp.float32)
        centred = values - jnp.mean(values, -1, keepdims=True)
        variance = jnp.mean(centred * centred, -1, keepdims=True)
        scaled = centred * lax.rsqrt(variance + 1e-05) * gain[...].astype(jnp.float32)
        normed[rows, :] = scaled.astype(jnp.bfloat16)
        return carry

    lax.fori_loop(0, tokens // norm_rows, normalise, 0)

    def iota(shape, axis):
        return lax.broadcasted_iota(jnp.int32, shape, axis)

    def ones_where(mask):
        return jnp.where(mask, 1.0, 0.0)

    square = (tokens, tokens)
    named_t = [routes_t[k : k + 1, :] == iota((experts, tokens), 0) for k in range(2)]
    earlier_t = jnp.dot(
        (ones_where(named_t[0]) + ones_where(named_t[1])).astype(jnp.bfloat16),
        ones_where(iota(square, 0) < iota(square, 1)).astype(jnp.bfloat16),
        preferred_element_type=jnp.float32,
    )
    rank_t = [jnp.sum(jnp.where(mask, earlier_t, 0.0), 0, keepdims=True) for mask in named_t]
    places = iota((cap, tokens), 0).astype(jnp.float32)

    def slot_rows(slot):
        expert = place(OFFSETS[slot], 1)[0]
        rank = jnp.where(
            routes_t[0:1, :] == expert, rank_t[0], jnp.where(routes_t[1:2, :] == expert, rank_t[1], -1.0)
        )
        return ones_where(rank == places)

    def dispatch(slot, part, side, where):
        columns = span(side * (SHARE + BOTH)) if part == 0 else pl.ds(SHARE, BOTH)
        source = outgoing.at[pl.ds(slot * cap, cap), columns]
        target = arrived.at[pl.ds(slot * cap, cap), columns]
        if slot == 0:
            return pltpu.make_async_copy(source, target, own_sem.at[part])
        number = part * experts + slot
        return remote(source, target, send_sem.at[number], recv_sem.at[number], where)

    sends = []

    def send(slot, part):
        index, side = place(OFFSETS[slot], 1)
        sends.append((slot, part, dispatch(slot, part, side, device(index, side))))
        sends[-1][2].start()

    blocks = slots // BLOCK
    per_block = BLOCK // cap
    for block in range(blocks):
        chosen = jnp.concatenate(
            [slot_rows(slot) for slot in range(block * per_block, (block + 1) * per_block)], 0
        ).astype(jnp.bfloat16)
        for start in range(0, width, SHARE):
            outgoing[block * BLOCK : (block + 1) * BLOCK, start : start + SHARE] = jnp.dot(
                chosen, normed[:, start : start + SHARE], preferred_element_type=jnp.float32
            ).astype(jnp.bfloat16)
        if block == 0:
            pl.semaphore_wait(barrier, len(greeted))
        for slot in range(block * per_block, (block + 1) * per_block):
            send(slot, 0)
    for slot in range(experts):
        send(slot, 1)

    logits_t = contract_rows(router_t[...], normed[...])

    def chosen_of(values, k):
        return jnp.sum(jnp.where(named_t[k], values, 0.0), 0, keepdims=True)

    def spot_of(k):
        return routes_t[k : k + 1, :].astype(jnp.float32) * cap + rank_t[k]

    leading_t = jax.nn.sigmoid(chosen_of(logits_t, 0) - chosen_of(logits_t, 1))
    rows_t = [spot_of(0), spot_of(1), leading_t, tgt_row[...].astype(jnp.float32)]
    token_columns = jnp.concatenate(rows_t + [jnp.zeros((4, tokens), jnp.float32)], 0).T
    spots = (token_columns[:, 0:1], token_columns[:, 1:2])
    gates = (token_columns[:, 2:3], 1.0 - token_columns[:, 2:3])
    matches = token_columns[:, 3:4] == src_row[...].astype(jnp.float32)
    match_rows[...] = ones_where(matches)
    for start in range(0, slots, BLOCK):
        columns = (iota((tokens, BLOCK), 1) + start).astype(jnp.float32)
        mixing = jnp.where(spots[0] == columns, gates[0], 0.0) + jnp.where(spots[1] == columns, gates[1], 0.0)
        rough = mixing.astype(jnp.bfloat16)
        coarse[:, start : start + BLOCK] = rough
        fine[:, start : start + BLOCK] = (mixing - rough.astype(jnp.float32)).astype(jnp.bfloat16)

    def wait_arrival(slot, part):
        if slot == 0:
            sends[0 if part == 0 else experts][2].wait()
        else:
            dispatch(slot, part, mp, partner).wait_recv()

    own_start = mp * (SHARE + BOTH)
    their_start = (1 - mp) * (SHARE + BOTH)

    def pass_on(number, start):
        region = arrived.at[pl.ds(number * GROUP, GROUP), span(start)]
        return remote(region, region, pass_sem.at[number], passed_sem.at[number], partner)

    groups = slots // GROUP
    per_group = GROUP // cap
    passes = [pass_on(number, own_start) for number in range(groups)]
    for number in range(groups):
        for slot in range(number * per_group, (number + 1) * per_group):
            wait_arrival(slot, 0)
        passes[number].start()

    def project(source, which, columns):
        return jnp.dot(source[:, columns], weight[which, columns, :], preferred_element_type=jnp.float32)

    for load in loads[:3]:
        load.wait()

    @pl.when(group == 1)
    def _():
        projected[1] = project(cotangent, 1, pl.ds(0, width))

    def tiles(count, step):
        def run(tile, carry):
            step(pl.ds(pl.multiple_of(tile * TILE, TILE), TILE))
            return carry

        lax.fori_loop(0, count // TILE, run, 0)

    def up_shared(block):
        rows = pl.ds(block * BLOCK, BLOCK)

        def step(columns):
            product = jnp.dot(
                arrived[rows, :SHARE], first[:SHARE, columns], preferred_element_type=jnp.float32
            ) + jnp.dot(
                arrived[rows, SHARE + BOTH :], first[SHARE + BOTH :, columns], preferred_element_type=jnp.float32
            )
            inner[rows, columns] = product.astype(jnp.bfloat16)

        tiles(inner.shape[1], step)

    def up_rest(block):
        rows = pl.ds(block * BLOCK, BLOCK)
        middle = pl.ds(SHARE, BOTH)

        def step(columns):
            product = jnp.dot(arrived[rows, middle], first[middle, columns], preferred_element_type=jnp.float32)
            total = product + inner[rows, columns].astype(jnp.float32)
            inner[rows, columns] = jnp.maximum(total, 0.0).astype(jnp.bfloat16)

        tiles(inner.shape[1], step)

    for block in range(blocks):
        for number in range(block * BLOCK // GROUP, (block + 1) * BLOCK // GROUP):
            pass_on(number, their_start).wait_recv()
        up_shared(block)

    def down_project(block, start, count, finish):
        rows = pl.ds(block * BLOCK, BLOCK)

        def step(tile, carry):
            columns = pl.ds(pl.multiple_of(start + tile * TILE, TILE), TILE)
            product = jnp.dot(inner[rows, :], second[:, columns], preferred_element_type=jnp.float32)
            finish(rows, pl.ds(pl.multiple_of(tile * TILE, TILE), TILE), product)
            return carry

        lax.fori_loop(0, count // TILE, step, 0)

    def keep_in(buffer):
        def finish(rows, columns, product):
            buffer[rows, columns] = product.astype(jnp.bfloat16)

        return finish

    def add_share(rows, columns, product):
        total = product + from_partner[rows, columns].astype(jnp.float32)
        share[rows, columns] = total.astype(jnp.bfloat16)

    def halve(block):
        rows = pl.ds(block * BLOCK, BLOCK)
        return remote(for_partner.at[rows], from_partner.at[rows], half_sem.at[block], halved_sem.at[block], partner)

    def give_back(slot, part, expert, where):
        start, count = (0, BOTH) if part == 0 else (BOTH + (part - 1) * LATE, LATE)
        rows = pl.ds(slot * cap, cap)
        source = both.at[rows] if part == 0 else share.at[rows, pl.ds(start - BOTH, LATE)]
        target = returned.at[pl.ds(pl.multiple_of(expert * cap, cap), cap), pl.ds(start, count)]
        if slot == 0:
            return pltpu.make_async_copy(source, target, own_sem.at[2 + part])
        number = part * experts + slot
        return remote(source, target, back_sem.at[number], came_sem.at[number], where)

    backs = []

    def give_block_back(block, part):
        for slot in range(block * per_block, (block + 1) * per_block):
            backs.append((slot, part, give_back(slot, part, row, device(*place(OFFSETS[slot], -1)))))
            backs[-1][2].start()

    loads[3].wait()
    halves = [halve(block) for block in range(blocks)]
    for block in range(blocks):
        for slot in range(block * per_block, (block + 1) * per_block):
            wait_arrival(slot, 1)
        up_rest(block)
        down_project(block, SHARE, BOTH, keep_in(both))
        give_block_back(block, 0)
        down_project(block, their_start, SHARE, keep_in(for_partner))
        halves[block].start()
    for block in range(blocks):
        halves[block].wait_recv()
        down_project(block, own_start, SHARE, add_share)
        give_block_back(block, 1)
    for block in range(blocks):
        give_block_back(block, 2)

    def mix_rows(rows, columns):
        values = returned[rows, columns]
        return jnp.dot(coarse[:, rows], values, preferred_element_type=jnp.float32) + jnp.dot(
            fine[:, rows], values, preferred_element_type=jnp.float32
        )

    def mix_part(part, mine):
        if part == 0:
            return mix_rows(pl.ds(0, slots), span((mp if mine else 1 - mp) * SHARE))
        which = row_h if mine else 1 - row_h
        return mix_rows(span(which * (slots // 2), slots // 2), pl.ds(BOTH + (part - 1) * LATE, LATE))

    def piece(part, side):
        if part == 0:
            return span(SHARE + side * SHARE)
        return pl.ds(pl.multiple_of(side * (SHARE + BOTH) + (part - 1) * LATE, LATE), LATE)

    parts = 1 + SHARE // LATE
    mix_columns = [pl.ds(0, SHARE)] + [pl.ds(SHARE + late * LATE, LATE) for late in range(parts - 1)]
    mixes = [
        remote(
            mix_out.at[:, columns], mix_in.at[:, columns], mix_sent.at[part], mix_here.at[part], partner
        )
        for part, columns in enumerate(mix_columns)
    ]

    def hand_state(part, side):
        region = state.at[:, piece(part, side)]
        return remote(region, region, state_sent.at[part], state_here.at[part], partner)

    hands = [hand_state(part, mp) for part in range(parts)]

    def project_piece(part, side, opening):
        columns = piece(part, side)
        term = project(state, 0, columns)
        projected[0] = term if opening else projected[0] + term

        @pl.when(group == 0)
        def _():
            other = project(state, 1, columns)
            projected[1] = other if opening else projected[1] + other

    for part in range(parts):
        for slot in range(experts):
            if slot > 0:
                give_back(slot, part, place(OFFSETS[slot], 1)[0], partner).wait_recv()
            else:
                backs[part * experts][2].wait()
        mix_out[:, mix_columns[part]] = mix_part(part, False).astype(jnp.bfloat16)
        mixes[part].start()
        own = mix_part(part, True)
        mixes[part].wait_recv()
        columns = piece(part, mp)
        total = hidden[:, columns].astype(jnp.float32) + (
            own + mix_in[:, mix_columns[part]].astype(jnp.float32)
        )
        state[:, columns] = total.astype(jnp.bfloat16)
        hands[part].start()
        project_piece(part, mp, part == 0)
    for part in range(parts):
        hand_state(part, 1 - mp).wait_recv()
        project_piece(part, 1 - mp, False)

    pair = 2 * HEAD_DIM
    for which in range(2):
        for heads in range(2):
            held[group, which, heads] = projected[which, :, heads * pair : (heads + 1) * pair].astype(
                jnp.bfloat16
            )

    def hand_held(which, owner, heads):
        region = held.at[owner, which, heads]
        return remote(region, region, held_sent.at[which], held_here.at[which], core)

    handed = [hand_held(which, group, 1 - group) for which in range(2)]
    for which in range(2):
        handed[which].start()
    matches = match_rows[...] > 0.0
    for which in range(2):
        hand_held(which, 1 - group, group).wait_recv()

    for head in range(2):
        columns = slice(head * HEAD_DIM, (head + 1) * HEAD_DIM)
        results = attend_head(
            held[1, 0, group][:, columns],
            held[0, 0, group][:, columns],
            held[0, 1, group][:, columns],
            held[1, 1, group][:, columns],
            matches,
        )
        for number, result in enumerate(results):
            grads[number // 2, number % 2, group, :, columns] = result

    def hand_grad(which, owner, heads):
        region = grads.at[owner, which, heads]
        return remote(region, region, grad_sent.at[which], grad_here.at[which], core)

    given = [hand_grad(which, 1 - group, group) for which in range(2)]
    for which in range(2):
        given[which].start()
    for which in range(2):
        hand_grad(which, group, 1 - group).wait_recv()

    def back_project(which, start):
        rows = span(start)
        return contract_rows(grads[group, which, 0], weight[which, rows, :pair]) + contract_rows(
            grads[group, which, 1], weight[which, rows, pair:]
        )

    def final(which, chunk):
        number = which * 2 + chunk
        return remote(
            final_out.at[number], final_in.at[number], final_sent.at[number], final_here.at[number], partner
        )

    @pl.when(group == 0)
    def _():
        for chunk in range(2):
            start = (1 - mp) * half + chunk * SHARE
            final_out[chunk] = (back_project(0, start) + back_project(1, start)).astype(jnp.bfloat16)
            final(0, chunk).start()
        forward[...] = state[:, span(mp * half, half)]
        for chunk in range(2):
            start = mp * half + chunk * SHARE
            own = back_project(0, start) + back_project(1, start)
            final(0, chunk).wait_recv()
            backward[:, chunk * SHARE : (chunk + 1) * SHARE] = (
                own + final_in[chunk].astype(jnp.float32)
            ).astype(jnp.bfloat16)
        for chunk in range(2):
            final(0, chunk).wait_send()

    @pl.when(group == 1)
    def _():
        for which in range(2):
            for chunk in range(2):
                start = (1 - mp) * half + chunk * SHARE
                final_out[which * 2 + chunk] = back_project(which, start).astype(jnp.bfloat16)
                final(which, chunk).start()
        for which, base, target in ((0, cotangent, backward), (1, state, forward)):
            for chunk in range(2):
                start = mp * half + chunk * SHARE
                own = back_project(which, start)
                final(which, chunk).wait_recv()
                total = base[:, span(start)].astype(jnp.float32) + (
                    own + final_in[which * 2 + chunk].astype(jnp.float32)
                )
                target[:, chunk * SHARE : (chunk + 1) * SHARE] = total.astype(jnp.bfloat16)
        for which in range(2):
            for chunk in range(2):
                final(which, chunk).wait_send()

    for slot, part, copy in sends + backs:
        if slot > 0:
            copy.wait_send()
    for copy in passes + halves + mixes + hands + handed + given:
        copy.wait_send()


def whole_layer(hidden, gain, router, routes, src_row, tgt_row, first, second, weight, cotangent):
    tokens, width = hidden.shape
    half, inner = width // 2, first.shape[1]
    experts = router.shape[1]
    slots = 4 * tokens
    pair = 2 * HEAD_DIM
    dma = pltpu.SemaphoreType.DMA
    vmem = pl.BlockSpec(memory_space=pltpu.VMEM)
    shapes = [
        (tokens, width),
        (slots, width),
        (slots, width),
        (slots, inner),
        first.shape,
        second.shape,
        weight.shape,
        cotangent.shape,
        (tokens, slots),
        (tokens, slots),
        (tokens, tokens, jnp.float32),
        (slots, SHARE),
        (slots, SHARE),
        (slots, BOTH),
        (slots, SHARE),
        (slots, BOTH + SHARE),
        (tokens, 2 * SHARE),
        (tokens, 2 * SHARE),
        (tokens, width),
        (2, tokens, 2 * pair, jnp.float32),
        (2, 2, 2, tokens, pair),
        (2, 2, 2, tokens, pair),
        (4, tokens, SHARE),
        (4, tokens, SHARE),
    ]
    scratch = [
        pltpu.VMEM(shape[:-1], shape[-1])
        if shape[-1] is jnp.float32
        else pltpu.VMEM(shape, jnp.bfloat16)
        for shape in shapes
    ]
    parts = 1 + SHARE // LATE
    counts = [4, 2 + parts] + [2 * experts] * 2 + [slots // GROUP] * 2 + [slots // BLOCK] * 2
    counts += [parts * experts] * 2 + [parts] * 4 + [2] * 4 + [4] * 2
    return pl.pallas_call(
        layer_kernel,
        out_shape=[jax.ShapeDtypeStruct((tokens, half), jnp.bfloat16)] * 2,
        in_specs=[vmem] * 6 + [pl.BlockSpec(memory_space=pl.ANY)] * 4,
        out_specs=[vmem] * 2,
        scratch_shapes=scratch + [dma((count,)) for count in counts],
        compiler_params=pltpu.CompilerParams(
            collective_id=0, has_side_effects=True, vmem_limit_bytes=60 * 1024 * 1024
        ),
        cost_estimate=pl.CostEstimate(
            flops=4 * slots * width * inner, bytes_accessed=24 * 1024 * 1024, transcendentals=131072
        ),
        name="whole_layer",
    )(
        hidden,
        gain,
        router.T,
        routes.T,
        src_row,
        tgt_row,
        first,
        second,
        weight,
        cotangent,
    )


def per_device(
    hidden_in,
    norm_gain,
    router,
    routes,
    expert_in,
    expert_out,
    attn_weight,
    src_segments,
    tgt_segments,
    cotangent,
):
    forward, backward = whole_layer(
        hidden_in[0],
        norm_gain,
        router[0],
        routes[0],
        src_segments,
        tgt_segments,
        expert_in[0, 0],
        expert_out[0, 0],
        attn_weight[0],
        cotangent,
    )
    return (forward[None], backward[None])


def solution(mesh):
    return jax.shard_map(
        per_device,
        mesh=mesh,
        in_specs=(
            P("grp", "dp", None),
            P("grp", None),
            P("grp", None, None),
            P("grp", "dp", None),
            P("grp", "dp", None, "mp"),
            P("grp", "dp", "mp", None),
            P("grp", None, None, "mp"),
            P("dp", None),
            P("dp", None),
            P("dp", None),
        ),
        out_specs=(P("grp", "dp", "mp"), P("grp", "dp", "mp")),
        check_vma=False,
    )
```

```python
import jax
import jax.numpy as jnp
from jax import lax
from jax.experimental import pallas as pl
from jax.experimental.pallas import tpu as pltpu
from jax.sharding import PartitionSpec as P

HEAD_DIM = 128


RINGS = (2, 4, 4)
SHARE = 512
BOTH = 1024
LATE = 256
GROUP = 128
BLOCK = 256
TILE = 256


def shortest(offset):
    return sum(min(step, ring - step) for step, ring in zip(offset, RINGS))


OFFSETS = sorted(
    [(h, z, y) for h in range(RINGS[0]) for z in range(RINGS[1]) for y in range(RINGS[2])],
    key=shortest,
)


def contract_rows(left_rows, weight):
    return lax.dot_general(
        left_rows, weight, (((1,), (1,)), ((), ())), preferred_element_type=jnp.float32
    )


def sum_rows(left, right):
    return lax.dot_general(left, right, (((0,), (0,)), ((), ())), preferred_element_type=jnp.float32)


def attend_head(query, key, value, grad, matches):
    softmax_scale = HEAD_DIM ** (-0.5)
    scores = contract_rows(query, key) * softmax_scale
    exp_scores = jnp.where(matches, jnp.exp(scores), 0.0)
    weights = exp_scores / jnp.sum(exp_scores, -1, keepdims=True)
    weights_b = weights.astype(jnp.bfloat16)
    context = jnp.dot(weights_b, value, preferred_element_type=jnp.float32)
    prob_grad = contract_rows(grad, value)
    row_delta = jnp.sum(weights * prob_grad, -1, keepdims=True)
    score_grad = (weights * (prob_grad - row_delta)).astype(jnp.bfloat16)
    query_grad = jnp.dot(score_grad, key, preferred_element_type=jnp.float32) * softmax_scale
    key_grad = sum_rows(score_grad, query) * softmax_scale
    value_grad = sum_rows(weights_b, grad)
    return [part.astype(jnp.bfloat16) for part in (key_grad, value_grad, query_grad, context)]


def layer_kernel(
    hidden,
    gain,
    router_t,
    routes_t,
    src_row,
    tgt_row,
    first_hbm,
    second_hbm,
    weight_hbm,
    cotangent_hbm,
    forward,
    backward,
    normed,
    outgoing,
    arrived,
    inner,
    first,
    second,
    weight,
    cotangent,
    coarse,
    fine,
    match_rows,
    for_partner,
    from_partner,
    both,
    share,
    returned,
    mix_out,
    mix_in,
    state,
    projected,
    held,
    grads,
    final_out,
    final_in,
    ahead,
    gathered,
    load_sem,
    own_sem,
    send_sem,
    recv_sem,
    pass_sem,
    passed_sem,
    half_sem,
    halved_sem,
    back_sem,
    came_sem,
    mix_sent,
    mix_here,
    state_sent,
    state_here,
    held_sent,
    held_here,
    grad_sent,
    grad_here,
    final_sent,
    final_here,
    ahead_sent,
    ahead_here,
    gather_sent,
    gather_here,
):
    group, row, mp = lax.axis_index("grp"), lax.axis_index("dp"), lax.axis_index("mp")
    experts = len(OFFSETS)
    slots, width = outgoing.shape
    tokens = hidden.shape[0]
    cap = slots // experts
    half = width // 2
    row_h, row_z, row_y = row // 16, row // 4 % 4, row % 4
    partner, core = {"mp": 1 - mp}, {"grp": 1 - group}
    across = {"grp": 1 - group, "mp": 1 - mp}
    decoder_across = {"grp": 1, "mp": 1 - mp}

    def place(offset, sign):
        dh, dz, dy = offset
        index = (
            (row_h + dh) % 2 * 16 + (row_z + sign * dz + 4) % 4 * 4 + (row_y + sign * dy + 4) % 4
        )
        return index, (mp + dh) % 2

    def device(index, side):
        return {"dp": index, "mp": side}

    def remote(source, target, sent, landed, where):
        return pltpu.make_async_remote_copy(
            source, target, sent, landed, device_id=where, device_id_type=pl.DeviceIdType.MESH
        )

    def span(start, count=SHARE):
        return pl.ds(pl.multiple_of(start, SHARE), count)

    barrier = pltpu.get_barrier_semaphore()
    greeted = [device(*place(offset, -1)) for offset in OFFSETS[1:]] + [partner, core, across]
    for where in greeted:
        pl.semaphore_signal(barrier, inc=1, device_id=where, device_id_type=pl.DeviceIdType.MESH)
    loads = [
        pltpu.make_async_copy(source, target, load_sem.at[number])
        for number, (source, target) in enumerate(
            ((first_hbm, first), (weight_hbm, weight), (cotangent_hbm, cotangent), (second_hbm, second))
        )
    ]

    norm_rows = 64

    def normalise(step, carry):
        rows = pl.ds(pl.multiple_of(step * norm_rows, norm_rows), norm_rows)
        values = hidden[rows, :].astype(jnp.float32)
        centred = values - jnp.mean(values, -1, keepdims=True)
        variance = jnp.mean(centred * centred, -1, keepdims=True)
        scaled = centred * lax.rsqrt(variance + 1e-05) * gain[...].astype(jnp.float32)
        normed[rows, :] = scaled.astype(jnp.bfloat16)
        return carry

    lax.fori_loop(0, tokens // norm_rows, normalise, 0)

    def iota(shape, axis):
        return lax.broadcasted_iota(jnp.int32, shape, axis)

    def ones_where(mask):
        return jnp.where(mask, 1.0, 0.0)

    square = (tokens, tokens)
    named_t = [routes_t[k : k + 1, :] == iota((experts, tokens), 0) for k in range(2)]
    earlier_t = jnp.dot(
        (ones_where(named_t[0]) + ones_where(named_t[1])).astype(jnp.bfloat16),
        ones_where(iota(square, 0) < iota(square, 1)).astype(jnp.bfloat16),
        preferred_element_type=jnp.float32,
    )
    rank_t = [jnp.sum(jnp.where(mask, earlier_t, 0.0), 0, keepdims=True) for mask in named_t]
    places = iota((cap, tokens), 0).astype(jnp.float32)

    def slot_rows(slot):
        expert = place(OFFSETS[slot], 1)[0]
        rank = jnp.where(
            routes_t[0:1, :] == expert, rank_t[0], jnp.where(routes_t[1:2, :] == expert, rank_t[1], -1.0)
        )
        return ones_where(rank == places)

    def dispatch(slot, part, side, where):
        columns = span(side * (SHARE + BOTH)) if part == 0 else pl.ds(SHARE, BOTH)
        source = outgoing.at[pl.ds(slot * cap, cap), columns]
        target = arrived.at[pl.ds(slot * cap, cap), columns]
        if slot == 0:
            return pltpu.make_async_copy(source, target, own_sem.at[part])
        number = part * experts + slot
        return remote(source, target, send_sem.at[number], recv_sem.at[number], where)

    sends = []

    def send(slot, part):
        index, side = place(OFFSETS[slot], 1)
        sends.append((slot, part, dispatch(slot, part, side, device(index, side))))
        sends[-1][2].start()

    def send_ahead(which, side):
        source = weight_hbm.at[which, span(side * half, half)]
        return remote(source, ahead.at[which], ahead_sent.at[which], ahead_here.at[which], partner)

    blocks = slots // BLOCK
    per_block = BLOCK // cap
    for block in range(blocks):
        chosen = jnp.concatenate(
            [slot_rows(slot) for slot in range(block * per_block, (block + 1) * per_block)], 0
        ).astype(jnp.bfloat16)
        for start in range(0, width, SHARE):
            outgoing[block * BLOCK : (block + 1) * BLOCK, start : start + SHARE] = jnp.dot(
                chosen, normed[:, start : start + SHARE], preferred_element_type=jnp.float32
            ).astype(jnp.bfloat16)
        if block == 0:
            pl.semaphore_wait(barrier, len(greeted))

            @pl.when(group == 1)
            def _():
                send_ahead(0, 1 - mp).start()

        for slot in range(block * per_block, (block + 1) * per_block):
            send(slot, 0)
    for slot in range(experts):
        send(slot, 1)
    for load in loads:
        load.start()

    logits_t = contract_rows(router_t[...], normed[...])

    def chosen_of(values, k):
        return jnp.sum(jnp.where(named_t[k], values, 0.0), 0, keepdims=True)

    def spot_of(k):
        return routes_t[k : k + 1, :].astype(jnp.float32) * cap + rank_t[k]

    leading_t = jax.nn.sigmoid(chosen_of(logits_t, 0) - chosen_of(logits_t, 1))
    rows_t = [spot_of(0), spot_of(1), leading_t, tgt_row[...].astype(jnp.float32)]
    token_columns = jnp.concatenate(rows_t + [jnp.zeros((4, tokens), jnp.float32)], 0).T
    spots = (token_columns[:, 0:1], token_columns[:, 1:2])
    gates = (token_columns[:, 2:3], 1.0 - token_columns[:, 2:3])
    matches = token_columns[:, 3:4] == src_row[...].astype(jnp.float32)
    match_rows[...] = ones_where(matches)
    for start in range(0, slots, BLOCK):
        columns = (iota((tokens, BLOCK), 1) + start).astype(jnp.float32)
        mixing = jnp.where(spots[0] == columns, gates[0], 0.0) + jnp.where(spots[1] == columns, gates[1], 0.0)
        rough = mixing.astype(jnp.bfloat16)
        coarse[:, start : start + BLOCK] = rough
        fine[:, start : start + BLOCK] = (mixing - rough.astype(jnp.float32)).astype(jnp.bfloat16)

    def wait_arrival(slot, part):
        if slot == 0:
            sends[0 if part == 0 else experts][2].wait()
        else:
            dispatch(slot, part, mp, partner).wait_recv()

    own_start = mp * (SHARE + BOTH)
    their_start = (1 - mp) * (SHARE + BOTH)

    def pass_on(number, start):
        region = arrived.at[pl.ds(number * GROUP, GROUP), span(start)]
        return remote(region, region, pass_sem.at[number], passed_sem.at[number], partner)

    groups = slots // GROUP
    per_group = GROUP // cap
    passes = [pass_on(number, own_start) for number in range(groups)]
    for number in range(groups):
        for slot in range(number * per_group, (number + 1) * per_group):
            wait_arrival(slot, 0)
        passes[number].start()

    @pl.when(group == 1)
    def _():
        send_ahead(1, 1 - mp).start()

    def project(source, which, columns):
        return jnp.dot(source[:, columns], weight[which, columns, :], preferred_element_type=jnp.float32)

    for load in loads[:3]:
        load.wait()

    @pl.when(group == 1)
    def _():
        projected[1] = project(cotangent, 1, pl.ds(0, width))

    def tiles(count, step):
        def run(tile, carry):
            step(pl.ds(pl.multiple_of(tile * TILE, TILE), TILE))
            return carry

        lax.fori_loop(0, count // TILE, run, 0)

    def up_shared(block):
        rows = pl.ds(block * BLOCK, BLOCK)

        def step(columns):
            product = jnp.dot(
                arrived[rows, :SHARE], first[:SHARE, columns], preferred_element_type=jnp.float32
            ) + jnp.dot(
                arrived[rows, SHARE + BOTH :], first[SHARE + BOTH :, columns], preferred_element_type=jnp.float32
            )
            inner[rows, columns] = product.astype(jnp.bfloat16)

        tiles(inner.shape[1], step)

    def up_rest(block):
        rows = pl.ds(block * BLOCK, BLOCK)
        middle = pl.ds(SHARE, BOTH)

        def step(columns):
            product = jnp.dot(arrived[rows, middle], first[middle, columns], preferred_element_type=jnp.float32)
            total = product + inner[rows, columns].astype(jnp.float32)
            inner[rows, columns] = jnp.maximum(total, 0.0).astype(jnp.bfloat16)

        tiles(inner.shape[1], step)

    for block in range(blocks):
        for number in range(block * BLOCK // GROUP, (block + 1) * BLOCK // GROUP):
            pass_on(number, their_start).wait_recv()
        up_shared(block)

    def down_project(block, start, count, finish):
        rows = pl.ds(block * BLOCK, BLOCK)

        def step(tile, carry):
            columns = pl.ds(pl.multiple_of(start + tile * TILE, TILE), TILE)
            product = jnp.dot(inner[rows, :], second[:, columns], preferred_element_type=jnp.float32)
            finish(rows, pl.ds(pl.multiple_of(tile * TILE, TILE), TILE), product)
            return carry

        lax.fori_loop(0, count // TILE, step, 0)

    def keep_in(buffer):
        def finish(rows, columns, product):
            buffer[rows, columns] = product.astype(jnp.bfloat16)

        return finish

    def add_share(rows, columns, product):
        total = product + from_partner[rows, columns].astype(jnp.float32)
        share[rows, columns] = total.astype(jnp.bfloat16)

    def halve(block):
        rows = pl.ds(block * BLOCK, BLOCK)
        return remote(for_partner.at[rows], from_partner.at[rows], half_sem.at[block], halved_sem.at[block], partner)

    def give_back(slot, part, expert, where):
        start, count = (0, BOTH) if part == 0 else (BOTH + (part - 1) * LATE, LATE)
        rows = pl.ds(slot * cap, cap)
        source = both.at[rows] if part == 0 else share.at[rows, pl.ds(start - BOTH, LATE)]
        target = returned.at[pl.ds(pl.multiple_of(expert * cap, cap), cap), pl.ds(start, count)]
        if slot == 0:
            return pltpu.make_async_copy(source, target, own_sem.at[2 + part])
        number = part * experts + slot
        return remote(source, target, back_sem.at[number], came_sem.at[number], where)

    backs = []

    def give_block_back(block, part):
        for slot in range(block * per_block, (block + 1) * per_block):
            backs.append((slot, part, give_back(slot, part, row, device(*place(OFFSETS[slot], -1)))))
            backs[-1][2].start()

    loads[3].wait()
    halves = [halve(block) for block in range(blocks)]
    for block in range(blocks):
        for slot in range(block * per_block, (block + 1) * per_block):
            wait_arrival(slot, 1)
        up_rest(block)
        down_project(block, SHARE, BOTH, keep_in(both))
        give_block_back(block, 0)
        down_project(block, their_start, SHARE, keep_in(for_partner))
        halves[block].start()
    for block in range(blocks):
        halves[block].wait_recv()
        down_project(block, own_start, SHARE, add_share)
        give_block_back(block, 1)
    for block in range(blocks):
        give_block_back(block, 2)

    def mix_rows(rows, columns):
        values = returned[rows, columns]
        return jnp.dot(coarse[:, rows], values, preferred_element_type=jnp.float32) + jnp.dot(
            fine[:, rows], values, preferred_element_type=jnp.float32
        )

    def mix_part(part, mine):
        if part == 0:
            return mix_rows(pl.ds(0, slots), span((mp if mine else 1 - mp) * SHARE))
        which = row_h if mine else 1 - row_h
        return mix_rows(span(which * (slots // 2), slots // 2), pl.ds(BOTH + (part - 1) * LATE, LATE))

    def piece(part, side):
        if part == 0:
            return span(SHARE + side * SHARE)
        return pl.ds(pl.multiple_of(side * (SHARE + BOTH) + (part - 1) * LATE, LATE), LATE)

    parts = 1 + SHARE // LATE
    mix_columns = [pl.ds(0, SHARE)] + [pl.ds(SHARE + late * LATE, LATE) for late in range(parts - 1)]
    mixes = [
        remote(
            mix_out.at[:, columns], mix_in.at[:, columns], mix_sent.at[part], mix_here.at[part], partner
        )
        for part, columns in enumerate(mix_columns)
    ]

    def hand_state(part, side):
        region = state.at[:, piece(part, side)]
        return remote(region, region, state_sent.at[part], state_here.at[part], partner)

    hands = [hand_state(part, mp) for part in range(parts)]

    def project_piece(part, side, opening):
        columns = piece(part, side)
        term = project(state, 0, columns)
        projected[0] = term if opening else projected[0] + term

        @pl.when(group == 0)
        def _():
            other = project(state, 1, columns)
            projected[1] = other if opening else projected[1] + other

    for part in range(parts):
        for slot in range(experts):
            if slot > 0:
                give_back(slot, part, place(OFFSETS[slot], 1)[0], partner).wait_recv()
            else:
                backs[part * experts][2].wait()
        mix_out[:, mix_columns[part]] = mix_part(part, False).astype(jnp.bfloat16)
        mixes[part].start()
        own = mix_part(part, True)
        mixes[part].wait_recv()
        columns = piece(part, mp)
        total = hidden[:, columns].astype(jnp.float32) + (
            own + mix_in[:, mix_columns[part]].astype(jnp.float32)
        )
        state[:, columns] = total.astype(jnp.bfloat16)
        hands[part].start()
        project_piece(part, mp, part == 0)
    for part in range(parts):
        hand_state(part, 1 - mp).wait_recv()
        project_piece(part, 1 - mp, False)

    pair = 2 * HEAD_DIM
    for which in range(2):
        for heads in range(2):
            held[group, which, heads] = projected[which, :, heads * pair : (heads + 1) * pair].astype(
                jnp.bfloat16
            )

    def hand_held(which, owner, heads):
        region = held.at[owner, which, heads]
        return remote(region, region, held_sent.at[which], held_here.at[which], core)

    handed = [hand_held(which, group, 1 - group) for which in range(2)]
    for which in range(2):
        handed[which].start()
    matches = match_rows[...] > 0.0
    for which in range(2):
        hand_held(which, 1 - group, group).wait_recv()

    for head in range(2):
        columns = slice(head * HEAD_DIM, (head + 1) * HEAD_DIM)
        results = attend_head(
            held[1, 0, group][:, columns],
            held[0, 0, group][:, columns],
            held[0, 1, group][:, columns],
            held[1, 1, group][:, columns],
            matches,
        )
        for number, result in enumerate(results):
            grads[number // 2, number % 2, group, :, columns] = result

    def hand_grad(which, owner, heads):
        region = grads.at[owner, which, heads]
        return remote(region, region, grad_sent.at[which], grad_here.at[which], core)

    given = [hand_grad(which, 1 - group, group) for which in range(2)]
    for which in range(2):
        given[which].start()

    def gather(which, heads):
        number = which * 2 + heads
        return remote(
            grads.at[1, which, heads],
            gathered.at[which, heads],
            gather_sent.at[which],
            gather_here.at[number],
            decoder_across,
        )

    gathers = [gather(which, group) for which in range(2)]
    for which in range(2):
        gathers[which].start()
    for which in range(2):
        hand_grad(which, group, 1 - group).wait_recv()

    def back_project(which, start):
        rows = span(start)
        return contract_rows(grads[group, which, 0], weight[which, rows, :pair]) + contract_rows(
            grads[group, which, 1], weight[which, rows, pair:]
        )

    def final(which, chunk):
        number = which * 2 + chunk
        return remote(
            final_out.at[number], final_in.at[number], final_sent.at[number], final_here.at[number], partner
        )

    @pl.when(group == 0)
    def _():
        for chunk in range(2):
            start = (1 - mp) * half + chunk * SHARE
            final_out[chunk] = (back_project(0, start) + back_project(1, start)).astype(jnp.bfloat16)
            final(0, chunk).start()
        forward[...] = state[:, span(mp * half, half)].astype(jnp.float32)
        for chunk in range(2):
            start = mp * half + chunk * SHARE
            own = back_project(0, start) + back_project(1, start)
            final(0, chunk).wait_recv()
            backward[:, chunk * SHARE : (chunk + 1) * SHARE] = (
                own + final_in[chunk].astype(jnp.float32)
            )
        for chunk in range(2):
            final(0, chunk).wait_send()

    @pl.when(group == 1)
    def _():
        for which in range(2):
            send_ahead(which, mp).wait_recv()
        for which, base, target in ((0, cotangent, backward), (1, state, forward)):
            own = [back_project(which, mp * half + chunk * SHARE) for chunk in range(2)]
            for heads in range(2):
                gather(which, heads).wait_recv()
            for chunk in range(2):
                rows = pl.ds(chunk * SHARE, SHARE)
                theirs = contract_rows(gathered[which, 0], ahead[which, rows, :pair]) + contract_rows(
                    gathered[which, 1], ahead[which, rows, pair:]
                )
                total = base[:, span(mp * half + chunk * SHARE)].astype(jnp.float32) + (own[chunk] + theirs)
                target[:, chunk * SHARE : (chunk + 1) * SHARE] = total
        for which in range(2):
            send_ahead(which, 1 - mp).wait_send()

    for slot, part, copy in sends + backs:
        if slot > 0:
            copy.wait_send()
    for copy in passes + halves + mixes + hands + handed + given + gathers:
        copy.wait_send()


def whole_layer(hidden, gain, router, routes, src_row, tgt_row, first, second, weight, cotangent):
    tokens, width = hidden.shape
    half, inner = width // 2, first.shape[1]
    experts = router.shape[1]
    slots = 4 * tokens
    pair = 2 * HEAD_DIM
    dma = pltpu.SemaphoreType.DMA
    vmem = pl.BlockSpec(memory_space=pltpu.VMEM)
    shapes = [
        (tokens, width),
        (slots, width),
        (slots, width),
        (slots, inner),
        first.shape,
        second.shape,
        weight.shape,
        cotangent.shape,
        (tokens, slots),
        (tokens, slots),
        (tokens, tokens, jnp.float32),
        (slots, SHARE),
        (slots, SHARE),
        (slots, BOTH),
        (slots, SHARE),
        (slots, BOTH + SHARE),
        (tokens, 2 * SHARE),
        (tokens, 2 * SHARE),
        (tokens, width),
        (2, tokens, 2 * pair, jnp.float32),
        (2, 2, 2, tokens, pair),
        (2, 2, 2, tokens, pair),
        (2, tokens, SHARE),
        (2, tokens, SHARE),
        (2, half, 2 * pair),
        (2, 2, tokens, pair),
    ]
    scratch = [
        pltpu.VMEM(shape[:-1], shape[-1])
        if shape[-1] is jnp.float32
        else pltpu.VMEM(shape, jnp.bfloat16)
        for shape in shapes
    ]
    parts = 1 + SHARE // LATE
    counts = [4, 2 + parts] + [2 * experts] * 2 + [slots // GROUP] * 2 + [slots // BLOCK] * 2
    counts += [parts * experts] * 2 + [parts] * 4 + [2] * 4 + [2] * 2 + [2] * 3 + [4]
    return pl.pallas_call(
        layer_kernel,
        out_shape=[jax.ShapeDtypeStruct((tokens, half), jnp.float32)] * 2,
        in_specs=[vmem] * 6 + [pl.BlockSpec(memory_space=pl.ANY)] * 4,
        out_specs=[vmem] * 2,
        scratch_shapes=scratch + [dma((count,)) for count in counts],
        compiler_params=pltpu.CompilerParams(
            collective_id=0, has_side_effects=True, vmem_limit_bytes=60 * 1024 * 1024
        ),
        cost_estimate=pl.CostEstimate(
            flops=4 * slots * width * inner, bytes_accessed=24 * 1024 * 1024, transcendentals=131072
        ),
        name="whole_layer",
    )(
        hidden,
        gain,
        router.T,
        routes.T,
        src_row,
        tgt_row,
        first,
        second,
        weight,
        cotangent,
    )


def per_device(
    hidden_in,
    norm_gain,
    router,
    routes,
    expert_in,
    expert_out,
    attn_weight,
    src_segments,
    tgt_segments,
    cotangent,
):
    forward, backward = whole_layer(
        hidden_in[0],
        norm_gain,
        router[0],
        routes[0],
        src_segments,
        tgt_segments,
        expert_in[0, 0],
        expert_out[0, 0],
        attn_weight[0],
        cotangent,
    )
    return (forward.astype(jnp.bfloat16)[None], backward.astype(jnp.bfloat16)[None])


def solution(mesh):
    return jax.shard_map(
        per_device,
        mesh=mesh,
        in_specs=(
            P("grp", "dp", None),
            P("grp", None),
            P("grp", None, None),
            P("grp", "dp", None),
            P("grp", "dp", None, "mp"),
            P("grp", "dp", "mp", None),
            P("grp", None, None, "mp"),
            P("dp", None),
            P("dp", None),
            P("dp", None),
        ),
        out_specs=(P("grp", "dp", "mp"), P("grp", "dp", "mp")),
        check_vma=False,
    )
```

```python
import jax
import jax.numpy as jnp
from jax import lax
from jax.experimental import pallas as pl
from jax.experimental.pallas import tpu as pltpu
from jax.sharding import PartitionSpec as P

HEAD_DIM = 128


RINGS = (2, 4, 4)
SHARE = 512
BOTH = 1024
LATE = 256
GROUP = 128
BLOCK = 256
TILE = 256


def shortest(offset):
    return sum(min(step, ring - step) for step, ring in zip(offset, RINGS))


OFFSETS = sorted(
    [(h, z, y) for h in range(RINGS[0]) for z in range(RINGS[1]) for y in range(RINGS[2])],
    key=shortest,
)


def contract_rows(left_rows, weight):
    return lax.dot_general(
        left_rows, weight, (((1,), (1,)), ((), ())), preferred_element_type=jnp.float32
    )


def sum_rows(left, right):
    return lax.dot_general(left, right, (((0,), (0,)), ((), ())), preferred_element_type=jnp.float32)


def attend_head(query, key, value, grad, matches):
    softmax_scale = HEAD_DIM ** (-0.5)
    scores = contract_rows(query, key) * softmax_scale
    exp_scores = jnp.where(matches, jnp.exp(scores), 0.0)
    weights = exp_scores / jnp.sum(exp_scores, -1, keepdims=True)
    weights_b = weights.astype(jnp.bfloat16)
    context = jnp.dot(weights_b, value, preferred_element_type=jnp.float32)
    prob_grad = contract_rows(grad, value)
    row_delta = jnp.sum(weights * prob_grad, -1, keepdims=True)
    score_grad = (weights * (prob_grad - row_delta)).astype(jnp.bfloat16)
    query_grad = jnp.dot(score_grad, key, preferred_element_type=jnp.float32) * softmax_scale
    key_grad = sum_rows(score_grad, query) * softmax_scale
    value_grad = sum_rows(weights_b, grad)
    return [part.astype(jnp.bfloat16) for part in (key_grad, value_grad, query_grad, context)]


def layer_kernel(
    hidden,
    gain,
    router_t,
    routes_t,
    src_row,
    tgt_row,
    first_hbm,
    second_hbm,
    weight_hbm,
    cotangent_hbm,
    forward,
    backward,
    normed,
    outgoing,
    arrived,
    inner,
    first,
    second,
    weight,
    cotangent,
    coarse,
    fine,
    match_rows,
    for_partner,
    from_partner,
    both,
    share,
    returned,
    mix_out,
    mix_in,
    state,
    projected,
    held,
    grads,
    final_out,
    final_in,
    ahead,
    gathered,
    load_sem,
    own_sem,
    send_sem,
    recv_sem,
    pass_sem,
    passed_sem,
    half_sem,
    halved_sem,
    back_sem,
    came_sem,
    mix_sent,
    mix_here,
    state_sent,
    state_here,
    held_sent,
    held_here,
    grad_sent,
    grad_here,
    final_sent,
    final_here,
    ahead_sent,
    ahead_here,
    gather_sent,
    gather_here,
):
    group, row, mp = lax.axis_index("grp"), lax.axis_index("dp"), lax.axis_index("mp")
    experts = len(OFFSETS)
    slots, width = outgoing.shape
    tokens = hidden.shape[0]
    cap = slots // experts
    half = width // 2
    row_h, row_z, row_y = row // 16, row // 4 % 4, row % 4
    partner, core = {"mp": 1 - mp}, {"grp": 1 - group}
    across = {"grp": 1 - group, "mp": 1 - mp}
    decoder_across = {"grp": 1, "mp": 1 - mp}

    def place(offset, sign):
        dh, dz, dy = offset
        index = (
            (row_h + dh) % 2 * 16 + (row_z + sign * dz + 4) % 4 * 4 + (row_y + sign * dy + 4) % 4
        )
        return index, (mp + dh) % 2

    def device(index, side):
        return {"dp": index, "mp": side}

    def remote(source, target, sent, landed, where):
        return pltpu.make_async_remote_copy(
            source, target, sent, landed, device_id=where, device_id_type=pl.DeviceIdType.MESH
        )

    def span(start, count=SHARE):
        return pl.ds(pl.multiple_of(start, SHARE), count)

    barrier = pltpu.get_barrier_semaphore()
    greeted = [device(*place(offset, -1)) for offset in OFFSETS[1:]] + [partner, core, across]
    for where in greeted:
        pl.semaphore_signal(barrier, inc=1, device_id=where, device_id_type=pl.DeviceIdType.MESH)
    loads = [
        pltpu.make_async_copy(source, target, load_sem.at[number])
        for number, (source, target) in enumerate(
            ((first_hbm, first), (weight_hbm, weight), (cotangent_hbm, cotangent), (second_hbm, second))
        )
    ]

    norm_rows = 64

    def normalise(step, carry):
        rows = pl.ds(pl.multiple_of(step * norm_rows, norm_rows), norm_rows)
        values = hidden[rows, :].astype(jnp.float32)
        centred = values - jnp.mean(values, -1, keepdims=True)
        variance = jnp.mean(centred * centred, -1, keepdims=True)
        scaled = centred * lax.rsqrt(variance + 1e-05) * gain[...].astype(jnp.float32)
        normed[rows, :] = scaled.astype(jnp.bfloat16)
        return carry

    lax.fori_loop(0, tokens // norm_rows, normalise, 0)

    def iota(shape, axis):
        return lax.broadcasted_iota(jnp.int32, shape, axis)

    def ones_where(mask):
        return jnp.where(mask, 1.0, 0.0)

    square = (tokens, tokens)
    named_t = [routes_t[k : k + 1, :] == iota((experts, tokens), 0) for k in range(2)]
    earlier_t = jnp.dot(
        (ones_where(named_t[0]) + ones_where(named_t[1])).astype(jnp.bfloat16),
        ones_where(iota(square, 0) < iota(square, 1)).astype(jnp.bfloat16),
        preferred_element_type=jnp.float32,
    )
    rank_t = [jnp.sum(jnp.where(mask, earlier_t, 0.0), 0, keepdims=True) for mask in named_t]
    places = iota((cap, tokens), 0).astype(jnp.float32)

    def slot_rows(slot):
        expert = place(OFFSETS[slot], 1)[0]
        rank = jnp.where(
            routes_t[0:1, :] == expert, rank_t[0], jnp.where(routes_t[1:2, :] == expert, rank_t[1], -1.0)
        )
        return ones_where(rank == places)

    def dispatch(slot, part, side, where):
        columns = span(side * (SHARE + BOTH)) if part == 0 else pl.ds(SHARE, BOTH)
        source = outgoing.at[pl.ds(slot * cap, cap), columns]
        target = arrived.at[pl.ds(slot * cap, cap), columns]
        if slot == 0:
            return pltpu.make_async_copy(source, target, own_sem.at[part])
        number = part * experts + slot
        return remote(source, target, send_sem.at[number], recv_sem.at[number], where)

    sends = []

    def send(slot, part):
        index, side = place(OFFSETS[slot], 1)
        sends.append((slot, part, dispatch(slot, part, side, device(index, side))))
        sends[-1][2].start()

    def send_ahead(which, side):
        source = weight_hbm.at[which, span(side * half, half)]
        return remote(source, ahead.at[which], ahead_sent.at[which], ahead_here.at[which], partner)

    blocks = slots // BLOCK
    per_block = BLOCK // cap
    for block in range(blocks):
        chosen = jnp.concatenate(
            [slot_rows(slot) for slot in range(block * per_block, (block + 1) * per_block)], 0
        ).astype(jnp.bfloat16)
        for start in range(0, width, SHARE):
            outgoing[block * BLOCK : (block + 1) * BLOCK, start : start + SHARE] = jnp.dot(
                chosen, normed[:, start : start + SHARE], preferred_element_type=jnp.float32
            ).astype(jnp.bfloat16)
        if block == 0:
            pl.semaphore_wait(barrier, len(greeted))

            @pl.when(group == 1)
            def _():
                send_ahead(0, 1 - mp).start()

        for slot in range(block * per_block, (block + 1) * per_block):
            send(slot, 0)
    for slot in range(experts):
        send(slot, 1)
    for load in loads:
        load.start()

    logits_t = contract_rows(router_t[...], normed[...])

    def chosen_of(values, k):
        return jnp.sum(jnp.where(named_t[k], values, 0.0), 0, keepdims=True)

    def spot_of(k):
        return routes_t[k : k + 1, :].astype(jnp.float32) * cap + rank_t[k]

    leading_t = jax.nn.sigmoid(chosen_of(logits_t, 0) - chosen_of(logits_t, 1))
    rows_t = [spot_of(0), spot_of(1), leading_t, tgt_row[...].astype(jnp.float32)]
    token_columns = jnp.concatenate(rows_t + [jnp.zeros((4, tokens), jnp.float32)], 0).T
    spots = (token_columns[:, 0:1], token_columns[:, 1:2])
    gates = (token_columns[:, 2:3], 1.0 - token_columns[:, 2:3])
    matches = token_columns[:, 3:4] == src_row[...].astype(jnp.float32)
    match_rows[...] = ones_where(matches)
    for start in range(0, slots, BLOCK):
        columns = (iota((tokens, BLOCK), 1) + start).astype(jnp.float32)
        mixing = jnp.where(spots[0] == columns, gates[0], 0.0) + jnp.where(spots[1] == columns, gates[1], 0.0)
        rough = mixing.astype(jnp.bfloat16)
        coarse[:, start : start + BLOCK] = rough
        fine[:, start : start + BLOCK] = (mixing - rough.astype(jnp.float32)).astype(jnp.bfloat16)

    def wait_arrival(slot, part):
        if slot == 0:
            sends[0 if part == 0 else experts][2].wait()
        else:
            dispatch(slot, part, mp, partner).wait_recv()

    own_start = mp * (SHARE + BOTH)
    their_start = (1 - mp) * (SHARE + BOTH)

    def pass_on(number, start):
        region = arrived.at[pl.ds(number * GROUP, GROUP), span(start)]
        return remote(region, region, pass_sem.at[number], passed_sem.at[number], partner)

    groups = slots // GROUP
    per_group = GROUP // cap
    passes = [pass_on(number, own_start) for number in range(groups)]
    for number in range(groups):
        for slot in range(number * per_group, (number + 1) * per_group):
            wait_arrival(slot, 0)
        passes[number].start()

    @pl.when(group == 1)
    def _():
        send_ahead(1, 1 - mp).start()

    def project(source, which, columns):
        return jnp.dot(source[:, columns], weight[which, columns, :], preferred_element_type=jnp.float32)

    for load in loads[:3]:
        load.wait()

    @pl.when(group == 1)
    def _():
        projected[1] = project(cotangent, 1, pl.ds(0, width))

    def tiles(count, step):
        def run(tile, carry):
            step(pl.ds(pl.multiple_of(tile * TILE, TILE), TILE))
            return carry

        lax.fori_loop(0, count // TILE, run, 0)

    def up_shared(block):
        rows = pl.ds(block * BLOCK, BLOCK)

        def step(columns):
            product = jnp.dot(
                arrived[rows, :SHARE], first[:SHARE, columns], preferred_element_type=jnp.float32
            ) + jnp.dot(
                arrived[rows, SHARE + BOTH :], first[SHARE + BOTH :, columns], preferred_element_type=jnp.float32
            )
            inner[rows, columns] = product.astype(jnp.bfloat16)

        tiles(inner.shape[1], step)

    def up_rest(block):
        rows = pl.ds(block * BLOCK, BLOCK)
        middle = pl.ds(SHARE, BOTH)

        def step(columns):
            product = jnp.dot(arrived[rows, middle], first[middle, columns], preferred_element_type=jnp.float32)
            total = product + inner[rows, columns].astype(jnp.float32)
            inner[rows, columns] = jnp.maximum(total, 0.0).astype(jnp.bfloat16)

        tiles(inner.shape[1], step)

    for block in range(blocks):
        for number in range(block * BLOCK // GROUP, (block + 1) * BLOCK // GROUP):
            pass_on(number, their_start).wait_recv()
        up_shared(block)

    def down_project(block, start, count, finish):
        rows = pl.ds(block * BLOCK, BLOCK)

        def step(tile, carry):
            columns = pl.ds(pl.multiple_of(start + tile * TILE, TILE), TILE)
            product = jnp.dot(inner[rows, :], second[:, columns], preferred_element_type=jnp.float32)
            finish(rows, pl.ds(pl.multiple_of(tile * TILE, TILE), TILE), product)
            return carry

        lax.fori_loop(0, count // TILE, step, 0)

    def keep_in(buffer):
        def finish(rows, columns, product):
            buffer[rows, columns] = product.astype(jnp.bfloat16)

        return finish

    def add_share(rows, columns, product):
        total = product + from_partner[rows, columns].astype(jnp.float32)
        share[rows, columns] = total.astype(jnp.bfloat16)

    def halve(block):
        rows = pl.ds(block * BLOCK, BLOCK)
        return remote(for_partner.at[rows], from_partner.at[rows], half_sem.at[block], halved_sem.at[block], partner)

    def give_back(slot, part, expert, where):
        start, count = (0, BOTH) if part == 0 else (BOTH + (part - 1) * LATE, LATE)
        rows = pl.ds(slot * cap, cap)
        source = both.at[rows] if part == 0 else share.at[rows, pl.ds(start - BOTH, LATE)]
        target = returned.at[pl.ds(pl.multiple_of(expert * cap, cap), cap), pl.ds(start, count)]
        if slot == 0:
            return pltpu.make_async_copy(source, target, own_sem.at[2 + part])
        number = part * experts + slot
        return remote(source, target, back_sem.at[number], came_sem.at[number], where)

    backs = []

    def give_block_back(block, part):
        for slot in range(block * per_block, (block + 1) * per_block):
            backs.append((slot, part, give_back(slot, part, row, device(*place(OFFSETS[slot], -1)))))
            backs[-1][2].start()

    loads[3].wait()
    halves = [halve(block) for block in range(blocks)]
    for block in range(blocks):
        for slot in range(block * per_block, (block + 1) * per_block):
            wait_arrival(slot, 1)
        up_rest(block)
        down_project(block, SHARE, BOTH, keep_in(both))
        give_block_back(block, 0)
        down_project(block, their_start, SHARE, keep_in(for_partner))
        halves[block].start()
    for block in range(blocks):
        halves[block].wait_recv()
        down_project(block, own_start, SHARE, add_share)
        give_block_back(block, 1)
    for block in range(blocks):
        give_block_back(block, 2)

    def mix_rows(rows, columns):
        values = returned[rows, columns]
        return jnp.dot(coarse[:, rows], values, preferred_element_type=jnp.float32) + jnp.dot(
            fine[:, rows], values, preferred_element_type=jnp.float32
        )

    def mix_part(part, mine):
        if part == 0:
            return mix_rows(pl.ds(0, slots), span((mp if mine else 1 - mp) * SHARE))
        which = row_h if mine else 1 - row_h
        return mix_rows(span(which * (slots // 2), slots // 2), pl.ds(BOTH + (part - 1) * LATE, LATE))

    def piece(part, side):
        if part == 0:
            return span(SHARE + side * SHARE)
        return pl.ds(pl.multiple_of(side * (SHARE + BOTH) + (part - 1) * LATE, LATE), LATE)

    parts = 1 + SHARE // LATE
    mix_columns = [pl.ds(0, SHARE)] + [pl.ds(SHARE + late * LATE, LATE) for late in range(parts - 1)]
    mixes = [
        remote(
            mix_out.at[:, columns], mix_in.at[:, columns], mix_sent.at[part], mix_here.at[part], partner
        )
        for part, columns in enumerate(mix_columns)
    ]

    def hand_state(part, side):
        region = state.at[:, piece(part, side)]
        return remote(region, region, state_sent.at[part], state_here.at[part], partner)

    hands = [hand_state(part, mp) for part in range(parts)]

    def project_piece(part, side, opening):
        columns = piece(part, side)
        term = project(state, 0, columns)
        projected[0] = term if opening else projected[0] + term

        @pl.when(group == 0)
        def _():
            other = project(state, 1, columns)
            projected[1] = other if opening else projected[1] + other

    def open_part(part):
        for slot in range(experts):
            if slot > 0:
                give_back(slot, part, place(OFFSETS[slot], 1)[0], partner).wait_recv()
            else:
                backs[part * experts][2].wait()
        mix_out[:, mix_columns[part]] = mix_part(part, False).astype(jnp.bfloat16)
        mixes[part].start()
        return mix_part(part, True)

    def close_part(part, own):
        mixes[part].wait_recv()
        columns = piece(part, mp)
        total = hidden[:, columns].astype(jnp.float32) + (
            own + mix_in[:, mix_columns[part]].astype(jnp.float32)
        )
        state[:, columns] = total.astype(jnp.bfloat16)
        hands[part].start()

    opened = open_part(0)
    for part in range(parts):
        if part > 0:
            project_piece(part - 1, mp, part == 1)
        following = open_part(part + 1) if part > 0 and part + 1 < parts else None
        close_part(part, opened)
        opened = following if part > 0 else open_part(1)
    project_piece(parts - 1, mp, False)
    for part in range(parts):
        hand_state(part, 1 - mp).wait_recv()
        project_piece(part, 1 - mp, False)

    pair = 2 * HEAD_DIM
    for which in range(2):
        for heads in range(2):
            held[group, which, heads] = projected[which, :, heads * pair : (heads + 1) * pair].astype(
                jnp.bfloat16
            )

    def hand_held(which, owner, heads):
        region = held.at[owner, which, heads]
        return remote(region, region, held_sent.at[which], held_here.at[which], core)

    handed = [hand_held(which, group, 1 - group) for which in range(2)]
    for which in range(2):
        handed[which].start()
    matches = match_rows[...] > 0.0
    for which in range(2):
        hand_held(which, 1 - group, group).wait_recv()

    for head in range(2):
        columns = slice(head * HEAD_DIM, (head + 1) * HEAD_DIM)
        results = attend_head(
            held[1, 0, group][:, columns],
            held[0, 0, group][:, columns],
            held[0, 1, group][:, columns],
            held[1, 1, group][:, columns],
            matches,
        )
        for number, result in enumerate(results):
            grads[number // 2, number % 2, group, :, columns] = result

    def hand_grad(which, owner, heads):
        region = grads.at[owner, which, heads]
        return remote(region, region, grad_sent.at[which], grad_here.at[which], core)

    given = [hand_grad(which, 1 - group, group) for which in range(2)]
    for which in range(2):
        given[which].start()

    def gather(which, heads):
        number = which * 2 + heads
        return remote(
            grads.at[1, which, heads],
            gathered.at[which, heads],
            gather_sent.at[which],
            gather_here.at[number],
            decoder_across,
        )

    gathers = [gather(which, group) for which in range(2)]
    for which in range(2):
        gathers[which].start()
    for which in range(2):
        hand_grad(which, group, 1 - group).wait_recv()

    def back_project(which, start):
        rows = span(start)
        return contract_rows(grads[group, which, 0], weight[which, rows, :pair]) + contract_rows(
            grads[group, which, 1], weight[which, rows, pair:]
        )

    def final(which, chunk):
        number = which * 2 + chunk
        return remote(
            final_out.at[number], final_in.at[number], final_sent.at[number], final_here.at[number], partner
        )

    @pl.when(group == 0)
    def _():
        for chunk in range(2):
            start = (1 - mp) * half + chunk * SHARE
            final_out[chunk] = (back_project(0, start) + back_project(1, start)).astype(jnp.bfloat16)
            final(0, chunk).start()
        forward[...] = state[:, span(mp * half, half)].astype(jnp.float32)
        for chunk in range(2):
            start = mp * half + chunk * SHARE
            own = back_project(0, start) + back_project(1, start)
            final(0, chunk).wait_recv()
            backward[:, chunk * SHARE : (chunk + 1) * SHARE] = (
                own + final_in[chunk].astype(jnp.float32)
            )
        for chunk in range(2):
            final(0, chunk).wait_send()

    @pl.when(group == 1)
    def _():
        for which in range(2):
            send_ahead(which, mp).wait_recv()
        for which, base, target in ((0, cotangent, backward), (1, state, forward)):
            own = [back_project(which, mp * half + chunk * SHARE) for chunk in range(2)]
            for heads in range(2):
                gather(which, heads).wait_recv()
            for chunk in range(2):
                rows = pl.ds(chunk * SHARE, SHARE)
                theirs = contract_rows(gathered[which, 0], ahead[which, rows, :pair]) + contract_rows(
                    gathered[which, 1], ahead[which, rows, pair:]
                )
                total = base[:, span(mp * half + chunk * SHARE)].astype(jnp.float32) + (own[chunk] + theirs)
                target[:, chunk * SHARE : (chunk + 1) * SHARE] = total
        for which in range(2):
            send_ahead(which, 1 - mp).wait_send()

    for slot, part, copy in sends + backs:
        if slot > 0:
            copy.wait_send()
    for copy in passes + halves + mixes + hands + handed + given + gathers:
        copy.wait_send()


def whole_layer(hidden, gain, router, routes, src_row, tgt_row, first, second, weight, cotangent):
    tokens, width = hidden.shape
    half, inner = width // 2, first.shape[1]
    experts = router.shape[1]
    slots = 4 * tokens
    pair = 2 * HEAD_DIM
    dma = pltpu.SemaphoreType.DMA
    vmem = pl.BlockSpec(memory_space=pltpu.VMEM)
    shapes = [
        (tokens, width),
        (slots, width),
        (slots, width),
        (slots, inner),
        first.shape,
        second.shape,
        weight.shape,
        cotangent.shape,
        (tokens, slots),
        (tokens, slots),
        (tokens, tokens, jnp.float32),
        (slots, SHARE),
        (slots, SHARE),
        (slots, BOTH),
        (slots, SHARE),
        (slots, BOTH + SHARE),
        (tokens, 2 * SHARE),
        (tokens, 2 * SHARE),
        (tokens, width),
        (2, tokens, 2 * pair, jnp.float32),
        (2, 2, 2, tokens, pair),
        (2, 2, 2, tokens, pair),
        (2, tokens, SHARE),
        (2, tokens, SHARE),
        (2, half, 2 * pair),
        (2, 2, tokens, pair),
    ]
    scratch = [
        pltpu.VMEM(shape[:-1], shape[-1])
        if shape[-1] is jnp.float32
        else pltpu.VMEM(shape, jnp.bfloat16)
        for shape in shapes
    ]
    parts = 1 + SHARE // LATE
    counts = [4, 2 + parts] + [2 * experts] * 2 + [slots // GROUP] * 2 + [slots // BLOCK] * 2
    counts += [parts * experts] * 2 + [parts] * 4 + [2] * 4 + [2] * 2 + [2] * 3 + [4]
    return pl.pallas_call(
        layer_kernel,
        out_shape=[jax.ShapeDtypeStruct((tokens, half), jnp.float32)] * 2,
        in_specs=[vmem] * 6 + [pl.BlockSpec(memory_space=pl.ANY)] * 4,
        out_specs=[vmem] * 2,
        scratch_shapes=scratch + [dma((count,)) for count in counts],
        compiler_params=pltpu.CompilerParams(
            collective_id=0, has_side_effects=True, vmem_limit_bytes=60 * 1024 * 1024
        ),
        cost_estimate=pl.CostEstimate(
            flops=4 * slots * width * inner, bytes_accessed=24 * 1024 * 1024, transcendentals=131072
        ),
        name="whole_layer",
    )(
        hidden,
        gain,
        router.T,
        routes.T,
        src_row,
        tgt_row,
        first,
        second,
        weight,
        cotangent,
    )


def per_device(
    hidden_in,
    norm_gain,
    router,
    routes,
    expert_in,
    expert_out,
    attn_weight,
    src_segments,
    tgt_segments,
    cotangent,
):
    forward, backward = whole_layer(
        hidden_in[0],
        norm_gain,
        router[0],
        routes[0],
        src_segments,
        tgt_segments,
        expert_in[0, 0],
        expert_out[0, 0],
        attn_weight[0],
        cotangent,
    )
    return (forward.astype(jnp.bfloat16)[None], backward.astype(jnp.bfloat16)[None])


def solution(mesh):
    return jax.shard_map(
        per_device,
        mesh=mesh,
        in_specs=(
            P("grp", "dp", None),
            P("grp", None),
            P("grp", None, None),
            P("grp", "dp", None),
            P("grp", "dp", None, "mp"),
            P("grp", "dp", "mp", None),
            P("grp", None, None, "mp"),
            P("dp", None),
            P("dp", None),
            P("dp", None),
        ),
        out_specs=(P("grp", "dp", "mp"), P("grp", "dp", "mp")),
        check_vma=False,
    )
```
